512 devices in a mesh: group: 16 (over y, x), dev: 32 (over z, core).
Axes of the slice: x: 4, y: 4, z: 16, core: 2. Of those that a mesh axis runs over, the one named last changes fastest.
Arguments:
- cam_jac: float32 [18, 2162688], P(None, ('group', 'dev')), may hold values from -1 to 1
- point_jac: float32 [6, 2162688], P(None, ('group', 'dev')), may hold values from -3 to 3
- residuals: float32 [2, 2162688], P(None, ('group', 'dev')), may hold values from -15 to 15
- obs_camera: int32 [2162688], P(('group', 'dev')), may hold values from 0 to 127
- obs_point: int32 [2162688], P(('group', 'dev')), may hold values from 0 to 1023
- obs_count: int32 [512, 33], P(('group', 'dev')), may hold values from 42 to 128, as said below
- cam_damp: float32 [9, 65536], P(None, ('group', 'dev')), may hold values from 0.3 to 3
- pt_damp: float32 [3, 524288], P(None, ('group', 'dev')), may hold values from 0.3 to 3
- partner_mask: int32 [32], P('dev'), may hold values from 1 to 15
Outputs:
- update: float32 [9, 65536], P(None, ('group', 'dev'))
- remainder: float32 [9, 65536], P(None, ('group', 'dev'))
The draws below stay inside these ranges and needn't reach their ends.
Inputs may be any that keep to these rules, and one draw needn't show every extreme that they name: `obs_count`: slots at or beyond a count are padding. Every device's row holds one count equal to 128. For each index d within a partition, partitions g and g XOR partner_mask[d] are matched.
All inputs are finite; a program needn't handle non-finite values.
Results may differ from the reference program's by a relative error of at most 0.0085.
Values sent between devices are 32-bit elements; how exact they have to be, the bound alone decides.
No kernel may reach another device: no remote copies, remote signals or barrier semaphores. Data moves between devices by JAX's collectives and lax.ppermute only.
A program may use at most 64 MiB of HBM per device.

```python
import math
import jax
import jax.numpy as jnp

CAM_DEV = 128
PT_DEV = 1024
SLOT = 128
ITERS = 2
NCAM = 65536
NPT = 524288
OBS = 2162688
N_GROUP = 16
N_DEV = 32
DEVICES = 512


def draw_residuals(key, part):
    key = jax.random.fold_in(key, 23)
    position = jnp.arange(OBS, dtype=jnp.float32) / OBS
    base = jnp.clip(jax.random.normal(key, (2, OBS), jnp.float32), -5.0, 5.0)
    return base * jnp.exp(jnp.log(3.0) * position)[None, :]


def draw_obs_count(key, part):
    key = jax.random.fold_in(key, 11)
    first_key, second_key = jax.random.split(key)
    lowest = max(1, SLOT // 3)
    counts = jax.random.randint(first_key, (DEVICES, N_DEV + 1), lowest, SLOT + 1)
    chosen = jax.random.randint(second_key, (DEVICES, 1), 0, N_DEV + 1)
    columns = jnp.arange(N_DEV + 1, dtype=jnp.int32)[None, :]
    return jnp.where(columns == chosen, SLOT, counts).astype(jnp.int32)


def set_ends(values, key, least, high):
    dims = values.shape
    spot = [jax.random.randint(jax.random.fold_in(key, axis), (), 0, dims[axis]) for axis in range(len(dims))]
    values = values.at[tuple(spot)].set(least)
    longest = dims.index(max(dims))
    spot[longest] = (spot[longest] + 1) % dims[longest]
    return values.at[tuple(spot)].set(high)


def block_scale(own_key, shape, shards, least, high):
    def one(dim, parts):
        steps = jax.random.uniform(jax.random.fold_in(jax.random.fold_in(own_key, 6), dim), (parts,), jnp.float32, least / len(shards), high / len(shards))
        return jnp.repeat(jnp.exp(steps), shape[dim] // parts).reshape((-1,) + (1,) * (len(shape) - dim - 1))

    level = one(*shards[0])
    for cut in shards[1:]:
        level = level * one(*cut)
    return level


def scatter_about(stream_key, dims, deviation, reach, shards=(), kind=jnp.bfloat16):
    level = block_scale(stream_key, dims, shards, -0.22, 0.18) if shards else 1.0
    result = jax.random.normal(stream_key, dims, jnp.float32) * deviation * level
    return jnp.minimum(jnp.maximum(result, -reach), reach).astype(kind)


def setup_inputs(seed: int = 0) -> dict:
    key_list = jax.random.split(jax.random.key(seed), 10)
    cam_jac = scatter_about(key_list[0], (18, OBS), (SLOT * (N_DEV + 1) // CAM_DEV) ** -0.5, 1.0, ((1, 512),), jnp.float32)
    point_jac = scatter_about(key_list[1], (6, OBS), (SLOT * (N_DEV + 1) // PT_DEV) ** -0.5, 3.0, ((1, 512),), jnp.float32)
    residuals = draw_residuals(jax.random.fold_in(key_list[9], 71), 0)
    obs_camera = set_ends(jax.random.randint(key_list[3], (OBS,), 0, CAM_DEV), jax.random.fold_in(key_list[3], 1), 0, CAM_DEV - 1).astype(jnp.int32)
    obs_point = set_ends(jax.random.randint(key_list[4], (OBS,), 0, PT_DEV), jax.random.fold_in(key_list[4], 1), 0, PT_DEV - 1).astype(jnp.int32)
    obs_count = draw_obs_count(jax.random.fold_in(key_list[9], 71), 0)
    cam_damp = jnp.clip(jnp.exp(math.log(3.0) - 2.3025851 * jax.random.uniform(key_list[6], (9, NCAM), jnp.float32) ** block_scale(key_list[6], (9, NCAM), ((1, 512),), -0.2, 0.2)), 0.3, 3.0)
    pt_damp = jnp.clip(jnp.exp(math.log(3.0) - 2.3025851 * jax.random.uniform(key_list[7], (3, NPT), jnp.float32) ** block_scale(key_list[7], (3, NPT), ((1, 512),), -0.2, 0.2)), 0.3, 3.0)
    partner_mask = set_ends(jax.random.randint(key_list[8], (N_DEV,), 1, N_GROUP), jax.random.fold_in(key_list[8], 1), 1, N_GROUP - 1).astype(jnp.int32)
    return dict(cam_jac=cam_jac, point_jac=point_jac, residuals=residuals, obs_camera=obs_camera, obs_point=obs_point, obs_count=obs_count, cam_damp=cam_damp, pt_damp=pt_damp, partner_mask=partner_mask)


def seg_rows(entries, indices, item_count):
    return jax.vmap(lambda single: jax.ops.segment_sum(single, indices, num_segments=item_count))(entries)


def cam_apply(cam_rows, cam_values):
    first_row = jnp.sum(cam_rows[0:9] * cam_values, axis=0)
    second_row = jnp.sum(cam_rows[9:18] * cam_values, axis=0)
    return jnp.stack([first_row, second_row])


def cam_spread(cam_rows, slot_values):
    return cam_rows[0:9] * slot_values[0:1] + cam_rows[9:18] * slot_values[1:2]


def point_apply(point_rows, point_values):
    first_row = jnp.sum(point_rows[0:3] * point_values, axis=0)
    second_row = jnp.sum(point_rows[3:6] * point_values, axis=0)
    return jnp.stack([first_row, second_row])


def point_spread(point_rows, slot_values):
    return point_rows[0:3] * slot_values[0:1] + point_rows[3:6] * slot_values[1:2]


def point_blocks(point_rows, point_ids, damping):
    item_count = damping.shape[1]
    summands = []
    for first_axis, second_axis in ((0, 0), (0, 1), (0, 2), (1, 1), (1, 2), (2, 2)):
        summands.append(point_rows[first_axis] * point_rows[second_axis] + point_rows[3 + first_axis] * point_rows[3 + second_axis])
    blocks = seg_rows(jnp.stack(summands), point_ids, item_count)
    nothing = jnp.zeros_like(damping[0])
    return blocks + jnp.stack([damping[0], nothing, nothing, damping[1], nothing, damping[2]])


def solve_three(blocks, source):
    cofactor_xx = blocks[3] * blocks[5] - blocks[4] * blocks[4]
    cofactor_xy = blocks[2] * blocks[4] - blocks[1] * blocks[5]
    cofactor_xz = blocks[1] * blocks[4] - blocks[2] * blocks[3]
    cofactor_yy = blocks[0] * blocks[5] - blocks[2] * blocks[2]
    cofactor_yz = blocks[1] * blocks[2] - blocks[0] * blocks[4]
    cofactor_zz = blocks[0] * blocks[3] - blocks[1] * blocks[1]
    determinant = blocks[0] * cofactor_xx + blocks[1] * cofactor_xy + blocks[2] * cofactor_xz
    first_out = cofactor_xx * source[0] + cofactor_xy * source[1] + cofactor_xz * source[2]
    second_out = cofactor_xy * source[0] + cofactor_yy * source[1] + cofactor_yz * source[2]
    third_out = cofactor_xz * source[0] + cofactor_yz * source[1] + cofactor_zz * source[2]
    return jnp.stack([first_out, second_out, third_out]) / determinant


def point_correct(point_rows, point_ids, blocks, moved, item_count):
    pulled = solve_three(blocks, seg_rows(point_spread(point_rows, moved), point_ids, item_count))
    return moved - point_apply(point_rows, pulled[:, point_ids])


def reference(cam_jac, point_jac, residuals, obs_camera, obs_point, obs_count, cam_damp, pt_damp, partner_mask):
    slot_total = (N_DEV + 1) * SLOT
    position = jnp.arange(OBS, dtype=jnp.int32)
    holder = position // slot_total
    within = position % slot_total
    block_id = within // SLOT
    live = (within % SLOT < obs_count[holder, block_id]).astype(jnp.float32)
    group_id = holder // N_DEV
    member_id = (holder % N_DEV).astype(jnp.int32)
    target = jnp.where(block_id < N_DEV, group_id * N_DEV + block_id,
                       jnp.bitwise_xor(group_id, partner_mask[member_id]) * N_DEV + member_id)
    camera_ids = (target * CAM_DEV + obs_camera).astype(jnp.int32)
    point_ids = (holder * PT_DEV + obs_point).astype(jnp.int32)
    cam_rows = cam_jac * live
    point_rows = point_jac * live
    blocks = point_blocks(point_rows, point_ids, pt_damp)
    reduced = point_correct(point_rows, point_ids, blocks, residuals, NPT)
    gradient = -seg_rows(cam_spread(cam_rows, reduced), camera_ids, NCAM)
    diagonal = cam_damp + seg_rows(cam_rows[0:9] ** 2 + cam_rows[9:18] ** 2, camera_ids, NCAM)
    precond = 1.0 / diagonal

    def schur(direction):
        moved = cam_apply(cam_rows, direction[:, camera_ids])
        kept = point_correct(point_rows, point_ids, blocks, moved, NPT)
        return cam_damp * direction + seg_rows(cam_spread(cam_rows, kept), camera_ids, NCAM)

    update = jnp.zeros_like(gradient)
    remainder = gradient
    scaled = precond * remainder
    direction = scaled
    norm_now = jnp.sum(remainder * scaled)
    for step_index in range(ITERS):
        image = schur(direction)
        step_size = norm_now / jnp.sum(direction * image)
        update = update + step_size * direction
        remainder = remainder - step_size * image
        if step_index + 1 < ITERS:
            scaled = precond * remainder
            norm_next = jnp.sum(remainder * scaled)
            direction = scaled + (norm_next / norm_now) * direction
            norm_now = norm_next
    return update, remainder
```

```python
import jax
import jax.numpy as jnp
from jax import lax
from jax.experimental import pallas as pl
from jax.experimental.pallas import tpu as pltpu
from jax.sharding import PartitionSpec as P

F32 = jnp.float32
BF16 = jnp.bfloat16
PAIRS = ((0, 0), (0, 1), (0, 2), (1, 1), (1, 2), (2, 2))


def one_hot(ids, count):
    rows = lax.broadcasted_iota(jnp.int32, (count, ids.shape[1]), 0)
    return jnp.where(rows == ids, 1.0, 0.0).astype(BF16)


def pieces(values, count):
    found = []
    for _ in range(count - 1):
        found.append(values.astype(BF16).astype(F32))
        values = values - found[-1]
    return found + [values]


def collect(values, chosen, count=2):
    m = values.shape[0]
    stacked = jnp.concatenate(pieces(values, count), 0).astype(BF16)
    sums = lax.dot_general(
        stacked, chosen, (((1,), (1,)), ((), ())), preferred_element_type=F32
    )
    total = sums[0:m]
    for i in range(1, count):
        total = total + sums[i * m : (i + 1) * m]
    return total


def fetch(items, chosen):
    stacked = jnp.concatenate(pieces(items, 2), 1).astype(BF16)
    return jnp.dot(
        stacked, jnp.concatenate([chosen, chosen], 0), preferred_element_type=F32
    )


def col_sum(values):
    return jnp.sum(values, axis=0, keepdims=True)


def total(values):
    return jnp.sum(values, keepdims=True)


def lane_blocks(row):
    out = row[:, 0:128]
    for b in range(1, row.shape[1] // 128):
        out = out + row[:, b * 128 : (b + 1) * 128]
    return out


def put_payload(in_ref, out_ref, first, second, extra):
    inner = in_ref.shape[1]
    in_ref[0:1, :] = first[:, :inner]
    in_ref[1:2, :] = second[:, :inner]
    in_ref[2:3, :] = jnp.concatenate([extra] * (inner // 128), 1)
    out_ref[0:1, :] = first[:, inner:]
    out_ref[1:2, :] = second[:, inner:]


def row_of(in_ref, group_ref, partner, r):
    return jnp.concatenate([in_ref[r : r + 1, :], group_ref[partner, r : r + 1, :]], 1)


def group_total(group_ref):
    row = jnp.zeros((1, 128), F32)
    for i in range(group_ref.shape[0]):
        row = row + group_ref[i, 2:3, :]
    return total(row)


def solve_points(inverse, sums):
    c = [inverse[8 * i : 8 * i + 8] for i in range(6)]
    g = [sums[8 * i : 8 * i + 8] for i in range(3)]
    return jnp.concatenate(
        [
            c[0] * g[0] + c[1] * g[1] + c[2] * g[2],
            c[1] * g[0] + c[3] * g[1] + c[4] * g[2],
            c[2] * g[0] + c[4] * g[1] + c[5] * g[2],
        ],
        0,
    )


def spread_points(placed, first, second):
    return jnp.concatenate(
        [
            placed[8 * r : 8 * r + 8] * first + placed[24 + 8 * r : 32 + 8 * r] * second
            for r in range(3)
        ],
        0,
    )


def pull_points(placed, pulled, first, second):
    v0 = placed[0:8] * pulled[0:8] + placed[8:16] * pulled[8:16] + placed[16:24] * pulled[16:24]
    v1 = placed[24:32] * pulled[0:8] + placed[32:40] * pulled[8:16] + placed[40:48] * pulled[16:24]
    return first - col_sum(v0), second - col_sum(v1)


def setup_kernel(
    count_ref, cam_ref, point_ref, res_ref, cam_id_ref, point_id_ref, damp_ref,
    in_ref, group_ref, placed_ref, inverse_ref,
):
    n = cam_ref.shape[1]
    inner = n - 128
    lanes = lax.broadcasted_iota(jnp.int32, (1, 128), 1)
    live = jnp.concatenate(
        [jnp.where(lanes < count_ref[0, b], 1.0, 0.0) for b in range(n // 128)], 1
    )
    ids = point_id_ref[...]
    chosen = one_hot(jnp.bitwise_and(ids, 127), 128)
    high = jnp.right_shift(ids, 7)
    digit = jnp.where(lax.broadcasted_iota(jnp.int32, (8, n), 0) == high, live, 0.0)
    for r in range(6):
        placed_ref[8 * r : 8 * r + 8, :] = digit * point_ref[r : r + 1, :]
    placed = placed_ref[...]
    part = [placed[8 * r : 8 * r + 8] for r in range(6)]
    first, second = res_ref[0:1, :], res_ref[1:2, :]
    squares = [part[a] * part[b] + part[3 + a] * part[3 + b] for a, b in PAIRS]
    blocks = collect(jnp.concatenate(squares, 0), chosen, 3)
    sums = collect(spread_points(placed, first, second), chosen)
    b = [blocks[8 * i : 8 * i + 8] for i in range(6)]
    for axis, entry in ((0, 0), (1, 3), (2, 5)):
        damp = damp_ref[axis : axis + 1, :]
        b[entry] = b[entry] + jnp.concatenate(
            [damp[:, 128 * h : 128 * h + 128] for h in range(8)], 0
        )
    cof = [
        b[3] * b[5] - b[4] * b[4],
        b[2] * b[4] - b[1] * b[5],
        b[1] * b[4] - b[2] * b[3],
        b[0] * b[5] - b[2] * b[2],
        b[1] * b[2] - b[0] * b[4],
        b[0] * b[3] - b[1] * b[1],
    ]
    det = b[0] * cof[0] + b[1] * cof[1] + b[2] * cof[2]
    inverse = jnp.concatenate([c / det for c in cof], 0)
    inverse_ref[...] = inverse
    pulled = fetch(solve_points(inverse, sums), chosen)
    first, second = pull_points(placed, pulled, first, second)
    rows = cam_ref[...] * live
    cam_ids = cam_id_ref[...].astype(F32)

    def put(ref, i, lo):
        hi = lo + 128
        ref[i, 0:18, :] = rows[:, lo:hi]
        ref[i, 18:19, :] = first[:, lo:hi]
        ref[i, 19:20, :] = second[:, lo:hi]
        ref[i, 20:21, :] = cam_ids[:, lo:hi]
        ref[i, 21:24, :] = jnp.zeros((3, 128), F32)

    for i in range(in_ref.shape[0]):
        put(in_ref, i, 128 * i)
    for i in range(group_ref.shape[0]):
        put(group_ref, i, inner)


def cam_rows_of(in_ref, group_ref, partner):
    blocks = [in_ref[i] for i in range(in_ref.shape[0])]
    return jnp.concatenate(blocks + [group_ref[partner]], 1)


def spread_cams(owned, first, second):
    row = lax.broadcasted_iota(jnp.int32, owned.shape, 0)
    return owned * jnp.where(row < 9, first, jnp.where(row < 18, second, 0.0))


def halves(sums):
    return sums[0:9] + sums[9:18]


def apply_cams(owned, values, chosen):
    twice = jnp.concatenate([values, values, jnp.zeros((6, 128), F32)], 0)
    product = owned * fetch(twice, chosen)
    row = lax.broadcasted_iota(jnp.int32, (8, owned.shape[1]), 0)
    middle = product[8:16]
    first = col_sum(product[0:8] + jnp.where(row == 0, middle, 0.0))
    second = col_sum(product[16:24] + jnp.where(row == 0, 0.0, middle))
    return first, second


def start_kernel(
    partner_ref, pay_in_ref, pay_group_ref, damp_ref,
    in_ref, out_ref, rem_ref, dir_ref, pre_ref,
):
    owned = cam_rows_of(pay_in_ref, pay_group_ref, partner_ref[0])
    chosen = one_hot(owned[20:21].astype(jnp.int32), 128)
    row = lax.broadcasted_iota(jnp.int32, owned.shape, 0)
    squares = jnp.where(row < 18, owned * owned, 0.0)
    terms = jnp.concatenate([spread_cams(owned, owned[18:19], owned[19:20]), squares], 0)
    sums = collect(terms, chosen)
    remainder = -halves(sums[0:24])
    precond = 1.0 / (damp_ref[...] + halves(sums[24:48]))
    direction = precond * remainder
    rem_ref[...] = remainder
    pre_ref[...] = precond
    dir_ref[...] = direction
    first, second = apply_cams(owned, direction, chosen)
    put_payload(in_ref, out_ref, first, second, col_sum(remainder * direction))


def point_first_kernel(
    partner_ref, got_in_ref, got_group_ref, placed_ref, point_id_ref, inverse_ref,
    cam_damp_ref, dir_ref,
    in_ref, out_ref, moved_ref, norm_ref,
):
    partner = partner_ref[0]
    first = row_of(got_in_ref, got_group_ref, partner, 0)
    second = row_of(got_in_ref, got_group_ref, partner, 1)
    moved_ref[0:1, :] = first
    moved_ref[1:2, :] = second
    norm_ref[...] = jnp.broadcast_to(group_total(got_group_ref), (1, 128))
    direction = dir_ref[...]
    point_side(
        placed_ref, point_id_ref, inverse_ref, cam_damp_ref, direction, first, second, in_ref, out_ref
    )


def point_next_kernel(
    partner_ref, got_in_ref, got_group_ref, placed_ref, point_id_ref, inverse_ref,
    cam_damp_ref, dir_ref, scaled_ref, moved_ref, norm_ref,
    in_ref, out_ref, next_dir_ref, next_norm_ref,
):
    partner = partner_ref[0]
    norm_next = group_total(got_group_ref)
    ratio = norm_next / norm_ref[0:1, 0:1]
    first = row_of(got_in_ref, got_group_ref, partner, 0) + ratio * moved_ref[0:1, :]
    second = row_of(got_in_ref, got_group_ref, partner, 1) + ratio * moved_ref[1:2, :]
    direction = scaled_ref[...] + ratio * dir_ref[...]
    next_dir_ref[...] = direction
    next_norm_ref[...] = jnp.broadcast_to(norm_next, (1, 128))
    point_side(
        placed_ref, point_id_ref, inverse_ref, cam_damp_ref, direction, first, second, in_ref, out_ref
    )


def point_side(
    placed_ref, point_id_ref, inverse_ref, cam_damp_ref, direction, first, second, in_ref, out_ref
):
    placed = placed_ref[...]
    chosen = one_hot(jnp.bitwise_and(point_id_ref[...], 127), 128)
    sums = collect(spread_points(placed, first, second), chosen)
    pulled = fetch(solve_points(inverse_ref[...], sums), chosen)
    kept0, kept1 = pull_points(placed, pulled, first, second)
    bend = lane_blocks(first * kept0 + second * kept1)
    bend = bend + col_sum(cam_damp_ref[...] * direction * direction)
    put_payload(in_ref, out_ref, kept0, kept1, bend)


def image_of(partner, got_in_ref, got_group_ref, owned, chosen, damp, direction):
    first = row_of(got_in_ref, got_group_ref, partner, 0)
    second = row_of(got_in_ref, got_group_ref, partner, 1)
    return damp * direction + halves(collect(spread_cams(owned, first, second), chosen))


def camera_kernel(
    partner_ref, got_in_ref, got_group_ref, pay_in_ref, pay_group_ref,
    damp_ref, dir_ref, rem_ref, pre_ref, norm_ref,
    in_ref, out_ref, update_ref, next_rem_ref, scaled_ref,
):
    partner = partner_ref[0]
    owned = cam_rows_of(pay_in_ref, pay_group_ref, partner)
    chosen = one_hot(owned[20:21].astype(jnp.int32), 128)
    direction = dir_ref[...]
    image = image_of(
        partner, got_in_ref, got_group_ref, owned, chosen, damp_ref[...], direction
    )
    step = norm_ref[0:1, 0:1] / group_total(got_group_ref)
    remainder = rem_ref[...] - step * image
    scaled = pre_ref[...] * remainder
    update_ref[...] = step * direction
    next_rem_ref[...] = remainder
    scaled_ref[...] = scaled
    first, second = apply_cams(owned, scaled, chosen)
    put_payload(in_ref, out_ref, first, second, col_sum(remainder * scaled))


def last_kernel(
    partner_ref, got_in_ref, got_group_ref, pay_in_ref, pay_group_ref,
    damp_ref, dir_ref, rem_ref, update_ref, norm_ref,
    next_update_ref, next_rem_ref,
):
    partner = partner_ref[0]
    owned = cam_rows_of(pay_in_ref, pay_group_ref, partner)
    chosen = one_hot(owned[20:21].astype(jnp.int32), 128)
    direction = dir_ref[...]
    image = image_of(
        partner, got_in_ref, got_group_ref, owned, chosen, damp_ref[...], direction
    )
    step = norm_ref[0:1, 0:1] / group_total(got_group_ref)
    next_update_ref[...] = update_ref[...] + step * direction
    next_rem_ref[...] = rem_ref[...] - step * image


def pair_kernel(got_ref, outer_ref, pair_ref):
    partial = lane_blocks(got_ref[2:3, :])
    for i in range(pair_ref.shape[0]):
        pair_ref[i, 0:2, :] = outer_ref[...]
        pair_ref[i, 2:3, :] = partial


def call(kernel, name, smem, shapes, *args):
    vmem = pl.BlockSpec(memory_space=pltpu.VMEM)
    scalar = pl.BlockSpec(memory_space=pltpu.SMEM)
    return pl.pallas_call(
        kernel,
        name=name,
        out_shape=[jax.ShapeDtypeStruct(shape, F32) for shape in shapes],
        in_specs=[scalar] * smem + [vmem] * (len(args) - smem),
        out_specs=[vmem] * len(shapes),
        compiler_params=pltpu.CompilerParams(vmem_limit_bytes=32 * 1024 * 1024),
    )(*args)


def exchange(inner, outer):
    got = lax.all_to_all(inner, "dev", split_axis=1, concat_axis=1, tiled=True)
    (pair,) = call(pair_kernel, "pair", 0, [(lax.axis_size("group"), 3, 128)], got, outer)
    return got, lax.all_to_all(pair, "group", split_axis=0, concat_axis=0, tiled=True)


def on_device(
    cam_jac, point_jac, residuals, obs_camera, obs_point, obs_count, cam_damp, pt_damp, partner_mask
):
    n = cam_jac.shape[1]
    inner = n - 128
    groups = lax.axis_size("group")
    partner = jnp.bitwise_xor(partner_mask, lax.axis_index("group").astype(jnp.int32))
    point_ids = obs_point[None]
    pay_in, pay_group, placed, inverse = call(
        setup_kernel, "setup", 1,
        [(inner // 128, 24, 128), (groups, 24, 128), (48, n), (48, 128)],
        obs_count, cam_jac, point_jac, residuals, obs_camera[None], point_ids, pt_damp,
    )
    pay_in = lax.all_to_all(pay_in, "dev", split_axis=0, concat_axis=0, tiled=True)
    pay_group = lax.all_to_all(pay_group, "group", split_axis=0, concat_axis=0, tiled=True)
    field = (9, 128)
    payload = [(3, inner), (2, 128)]
    to_in, to_out, remainder, direction, precond = call(
        start_kernel, "start", 1, payload + [field] * 3, partner, pay_in, pay_group, cam_damp
    )
    got_in, got_group = exchange(to_in, to_out)
    to_in, to_out, moved, norm = call(
        point_first_kernel, "point_first", 1, payload + [(2, n), (1, 128)],
        partner, got_in, got_group, placed, point_ids, inverse, cam_damp, direction,
    )
    got_in, got_group = exchange(to_in, to_out)
    to_in, to_out, update, remainder, scaled = call(
        camera_kernel, "camera", 1, payload + [field] * 3,
        partner, got_in, got_group, pay_in, pay_group, cam_damp, direction, remainder, precond, norm,
    )
    got_in, got_group = exchange(to_in, to_out)
    to_in, to_out, direction, norm = call(
        point_next_kernel, "point_next", 1, payload + [field, (1, 128)],
        partner, got_in, got_group, placed, point_ids, inverse, cam_damp, direction, scaled, moved, norm,
    )
    got_in, got_group = exchange(to_in, to_out)
    update, remainder = call(
        last_kernel, "last", 1, [field] * 2,
        partner, got_in, got_group, pay_in, pay_group, cam_damp, direction, remainder, update, norm,
    )
    return (update, remainder)


def solution(mesh):
    slots, rows = P(None, ("group", "dev")), P(("group", "dev"))
    return jax.shard_map(
        on_device,
        mesh=mesh,
        in_specs=(
            slots, slots, slots, rows, rows, P(("group", "dev"), None), slots, slots, P("dev"),
        ),
        out_specs=(slots, slots),
        check_vma=False,
    )
```

```python
import jax
import jax.numpy as jnp
from jax import lax
from jax.experimental import pallas as pl
from jax.experimental.pallas import tpu as pltpu
from jax.sharding import PartitionSpec as P

F32 = jnp.float32
BF16 = jnp.bfloat16
PAIRS = ((0, 0), (0, 1), (0, 2), (1, 1), (1, 2), (2, 2))


def one_hot(ids, count):
    rows = lax.broadcasted_iota(jnp.int32, (count, ids.shape[1]), 0)
    return jnp.where(rows == ids, 1.0, 0.0).astype(BF16)


def pieces(values, count):
    found = []
    for _ in range(count - 1):
        found.append(values.astype(BF16).astype(F32))
        values = values - found[-1]
    return found + [values]


def collect(values, chosen, count=2):
    m = values.shape[0]
    stacked = jnp.concatenate(pieces(values, count), 0).astype(BF16)
    sums = lax.dot_general(
        stacked, chosen, (((1,), (1,)), ((), ())), preferred_element_type=F32
    )
    total = sums[0:m]
    for i in range(1, count):
        total = total + sums[i * m : (i + 1) * m]
    return total


def fetch(items, chosen):
    stacked = jnp.concatenate(pieces(items, 2), 1).astype(BF16)
    return jnp.dot(
        stacked, jnp.concatenate([chosen, chosen], 0), preferred_element_type=F32
    )


def col_sum(values):
    return jnp.sum(values, axis=0, keepdims=True)


def total(values):
    return jnp.sum(values, keepdims=True)


def lane_blocks(row):
    out = row[:, 0:128]
    for b in range(1, row.shape[1] // 128):
        out = out + row[:, b * 128 : (b + 1) * 128]
    return out


def scalar_row(values):
    lanes = lax.broadcasted_iota(jnp.int32, (1, 128), 1)
    row = jnp.broadcast_to(values[0], (1, 128))
    for i in range(1, len(values)):
        row = jnp.where(lanes < 32 * i, row, values[i])
    return row


def scalars(row, count):
    return [row[:, 32 * i : 32 * i + 1] for i in range(count)]


def put_rows(ref, rows):
    for r, row in enumerate(rows):
        ref[r : r + 1, :] = row


def repeat(row, width):
    return jnp.concatenate([row] * (width // 128), 1)


def with_outer(in_ref, out_ref, r):
    return jnp.concatenate([in_ref[r : r + 1, :], out_ref[r : r + 1, :]], 1)


def solve_points(inverse, sums):
    c = [inverse[8 * i : 8 * i + 8] for i in range(6)]
    g = [sums[8 * i : 8 * i + 8] for i in range(3)]
    return jnp.concatenate(
        [
            c[0] * g[0] + c[1] * g[1] + c[2] * g[2],
            c[1] * g[0] + c[3] * g[1] + c[4] * g[2],
            c[2] * g[0] + c[4] * g[1] + c[5] * g[2],
        ],
        0,
    )


def spread_points(placed, first, second):
    return jnp.concatenate(
        [
            placed[8 * r : 8 * r + 8] * first + placed[24 + 8 * r : 32 + 8 * r] * second
            for r in range(3)
        ],
        0,
    )


def pull_points(placed, pulled, first, second):
    v0 = placed[0:8] * pulled[0:8] + placed[8:16] * pulled[8:16] + placed[16:24] * pulled[16:24]
    v1 = placed[24:32] * pulled[0:8] + placed[32:40] * pulled[8:16] + placed[40:48] * pulled[16:24]
    return first - col_sum(v0), second - col_sum(v1)


def setup_kernel(
    count_ref, cam_ref, point_ref, res_ref, cam_id_ref, point_id_ref, damp_ref,
    in_ref, outer_ref, outer_sum_ref, placed_ref, inverse_ref,
):
    n = cam_ref.shape[1]
    inner = n - 128
    lanes = lax.broadcasted_iota(jnp.int32, (1, 128), 1)
    live = jnp.concatenate(
        [jnp.where(lanes < count_ref[0, b], 1.0, 0.0) for b in range(n // 128)], 1
    )
    ids = point_id_ref[...]
    chosen = one_hot(jnp.bitwise_and(ids, 127), 128)
    high = jnp.right_shift(ids, 7)
    digit = jnp.where(lax.broadcasted_iota(jnp.int32, (8, n), 0) == high, live, 0.0)
    for r in range(6):
        placed_ref[8 * r : 8 * r + 8, :] = digit * point_ref[r : r + 1, :]
    placed = placed_ref[...]
    part = [placed[8 * r : 8 * r + 8] for r in range(6)]
    first, second = res_ref[0:1, :], res_ref[1:2, :]
    squares = [part[a] * part[b] + part[3 + a] * part[3 + b] for a, b in PAIRS]
    blocks = collect(jnp.concatenate(squares, 0), chosen, 3)
    sums = collect(spread_points(placed, first, second), chosen)
    b = [blocks[8 * i : 8 * i + 8] for i in range(6)]
    for axis, entry in ((0, 0), (1, 3), (2, 5)):
        damp = damp_ref[axis : axis + 1, :]
        b[entry] = b[entry] + jnp.concatenate(
            [damp[:, 128 * h : 128 * h + 128] for h in range(8)], 0
        )
    cof = [
        b[3] * b[5] - b[4] * b[4],
        b[2] * b[4] - b[1] * b[5],
        b[1] * b[4] - b[2] * b[3],
        b[0] * b[5] - b[2] * b[2],
        b[1] * b[2] - b[0] * b[4],
        b[0] * b[3] - b[1] * b[1],
    ]
    det = b[0] * cof[0] + b[1] * cof[1] + b[2] * cof[2]
    inverse = jnp.concatenate([c / det for c in cof], 0)
    inverse_ref[...] = inverse
    pulled = fetch(solve_points(inverse, sums), chosen)
    first, second = pull_points(placed, pulled, first, second)
    rows = cam_ref[...] * live
    cam_ids = cam_id_ref[...].astype(F32)

    def put(ref, lo):
        hi = lo + 128
        ref[0:18, :] = rows[:, lo:hi]
        ref[18:19, :] = first[:, lo:hi]
        ref[19:20, :] = second[:, lo:hi]
        ref[20:21, :] = cam_ids[:, lo:hi]
        ref[21:24, :] = jnp.zeros((3, 128), F32)

    for i in range(in_ref.shape[0]):
        put(in_ref.at[i], 128 * i)
    put(outer_ref, inner)
    outer_sum_ref[...] = start_sums(outer_ref[...])


def spread_cams(owned, first, second):
    row = lax.broadcasted_iota(jnp.int32, owned.shape, 0)
    return owned * jnp.where(row < 9, first, jnp.where(row < 18, second, 0.0))


def halves(sums):
    return sums[0:9] + sums[9:18]


def apply_cams(owned, values, chosen):
    twice = jnp.concatenate([values, values, jnp.zeros((6, 128), F32)], 0)
    product = owned * fetch(twice, chosen)
    row = lax.broadcasted_iota(jnp.int32, (8, owned.shape[1]), 0)
    middle = product[8:16]
    first = col_sum(product[0:8] + jnp.where(row == 0, middle, 0.0))
    second = col_sum(product[16:24] + jnp.where(row == 0, 0.0, middle))
    return first, second


def ids_of(owned):
    return one_hot(owned[20:21].astype(jnp.int32), 128)


def start_sums(owned):
    row = lax.broadcasted_iota(jnp.int32, owned.shape, 0)
    squares = jnp.where(row < 18, owned * owned, 0.0)
    terms = jnp.concatenate([spread_cams(owned, owned[18:19], owned[19:20]), squares], 0)
    sums = collect(terms, ids_of(owned))
    return jnp.concatenate([halves(sums[0:24]), halves(sums[24:48])], 0)


def blocks_of(pay_ref):
    return jnp.concatenate([pay_ref[i] for i in range(pay_ref.shape[0])], 1)


def start_sum_kernel(pay_ref, outer_sum_ref, damp_ref, group_ref):
    sums = start_sums(blocks_of(pay_ref))
    for i in range(group_ref.shape[0]):
        group_ref[i, 0:9, :] = sums[0:9]
        group_ref[i, 9:18, :] = sums[9:18] + damp_ref[...]
        group_ref[i, 18:36, :] = outer_sum_ref[...]


def put_moved(in_ref, out_ref, pay_ref, outer_ref, own, twin):
    owned = blocks_of(pay_ref)
    put_rows(in_ref, apply_cams(owned, own, ids_of(owned)))
    outer = outer_ref[...]
    put_rows(out_ref, apply_cams(outer, twin, ids_of(outer)))


def start_kernel(
    partner_ref, group_ref, outer_sum_ref, pay_ref, outer_ref,
    in_ref, out_ref, rem_ref, pre_ref, dir_ref,
):
    theirs = group_ref[partner_ref[0]]
    mine = group_ref[partner_ref[1]]
    sums = [mine[0:18] + theirs[18:36], theirs[0:18] + outer_sum_ref[...]]
    for i in range(2):
        remainder = -sums[i][0:9]
        precond = 1.0 / sums[i][9:18]
        rem_ref[i] = remainder
        pre_ref[i] = precond
        dir_ref[i] = precond * remainder
    put_moved(in_ref, out_ref, pay_ref, outer_ref, dir_ref[0], dir_ref[1])


def point_side(in_ref, out_ref, placed_ref, point_id_ref, inverse_ref):
    placed = placed_ref[...]
    first, second = with_outer(in_ref, out_ref, 0), with_outer(in_ref, out_ref, 1)
    chosen = one_hot(jnp.bitwise_and(point_id_ref[...], 127), 128)
    sums = collect(spread_points(placed, first, second), chosen)
    pulled = fetch(solve_points(inverse_ref[...], sums), chosen)
    kept = pull_points(placed, pulled, first, second)
    return kept, total(lane_blocks(first * kept[0] + second * kept[1]))


def put_kept(back_ref, outer_sum_ref, outer_ref, kept, values):
    inner = back_ref.shape[1]
    put_rows(back_ref, [kept[0][:, :inner], kept[1][:, :inner], repeat(scalar_row(values), inner)])
    outer = outer_ref[...]
    spread = spread_cams(outer, kept[0][:, inner:], kept[1][:, inner:])
    outer_sum_ref[...] = halves(collect(spread, ids_of(outer)))


def point_first_kernel(
    in_ref, out_ref, placed_ref, point_id_ref, inverse_ref, outer_ref, damp_ref, rem_ref, dir_ref,
    back_ref, outer_sum_ref,
):
    kept, bend = point_side(in_ref, out_ref, placed_ref, point_id_ref, inverse_ref)
    direction = dir_ref[0]
    bend = bend + total(damp_ref[...] * direction * direction)
    put_kept(back_ref, outer_sum_ref, outer_ref, kept, [total(rem_ref[0] * direction), bend])


def point_next_kernel(
    in_ref, out_ref, placed_ref, point_id_ref, inverse_ref, outer_ref, damp_ref,
    rem_ref, scaled_ref, image_ref,
    back_ref, outer_sum_ref,
):
    kept, bend = point_side(in_ref, out_ref, placed_ref, point_id_ref, inverse_ref)
    scaled = scaled_ref[0]
    bend = bend + total(damp_ref[...] * scaled * scaled)
    values = [total(rem_ref[0] * scaled), bend, total(image_ref[...] * scaled)]
    put_kept(back_ref, outer_sum_ref, outer_ref, kept, values)


def inner_image(back_ref, pay_ref, damp_ref, field):
    owned = blocks_of(pay_ref)
    spread = spread_cams(owned, back_ref[0:1, :], back_ref[1:2, :])
    return damp_ref[...] * field + halves(collect(spread, ids_of(owned)))


def image_kernel(back_ref, outer_sum_ref, pay_ref, damp_ref, dir_ref, group_ref):
    image = inner_image(back_ref, pay_ref, damp_ref, dir_ref[0])
    partial = lane_blocks(back_ref[2:3, :])
    for i in range(group_ref.shape[0]):
        group_ref[i, 0:9, :] = image
        group_ref[i, 9:18, :] = outer_sum_ref[...]
        group_ref[i, 18:19, :] = partial


def group_total(group_ref, r):
    row = group_ref[0, r : r + 1, :]
    for i in range(1, group_ref.shape[0]):
        row = row + group_ref[i, r : r + 1, :]
    return row


def camera_kernel(
    partner_ref, group_ref, outer_sum_ref, pay_ref, outer_ref, rem_ref, pre_ref, dir_ref,
    in_ref, out_ref, next_rem_ref, scaled_ref, image_ref, sums_ref,
):
    sums = group_total(group_ref, 18)
    sums_ref[...] = sums
    norm, bend = scalars(sums, 2)
    step = norm / bend
    theirs = group_ref[partner_ref[0]]
    mine = group_ref[partner_ref[1]]
    images = [mine[0:9] + theirs[9:18], theirs[0:9] + outer_sum_ref[...]]
    image_ref[...] = images[0]
    for i in range(2):
        remainder = rem_ref[i] - step * images[i]
        next_rem_ref[i] = remainder
        scaled_ref[i] = pre_ref[i] * remainder
    put_moved(in_ref, out_ref, pay_ref, outer_ref, scaled_ref[0], scaled_ref[1])


def pair_kernel(back_ref, outer_sum_ref, group_ref):
    partial = lane_blocks(back_ref[2:3, :])
    for i in range(group_ref.shape[0]):
        group_ref[i, 0:9, :] = outer_sum_ref[...]
        group_ref[i, 9:10, :] = partial


def inner_kernel(back_ref, pay_ref, damp_ref, scaled_ref, image_ref):
    image_ref[...] = inner_image(back_ref, pay_ref, damp_ref, scaled_ref[0])


def last_kernel(
    partner_ref, group_ref, inner_ref, rem_ref, scaled_ref, dir_ref, image_ref, sums_ref,
    update_ref, next_rem_ref,
):
    norm, bend = scalars(sums_ref[...], 2)
    next_norm, next_bend, cross = scalars(group_total(group_ref, 9), 3)
    ratio = next_norm / norm
    next_bend = next_bend + ratio * (2.0 * cross + ratio * bend)
    step = next_norm / next_bend
    image = inner_ref[...] + group_ref[partner_ref[0], 0:9, :] + ratio * image_ref[...]
    direction = dir_ref[0]
    update_ref[...] = norm / bend * direction + step * (scaled_ref[0] + ratio * direction)
    next_rem_ref[...] = rem_ref[0] - step * image


def call(kernel, name, smem, shapes, *args):
    vmem = pl.BlockSpec(memory_space=pltpu.VMEM)
    scalar = pl.BlockSpec(memory_space=pltpu.SMEM)
    return pl.pallas_call(
        kernel,
        name=name,
        out_shape=[jax.ShapeDtypeStruct(shape, F32) for shape in shapes],
        in_specs=[scalar] * smem + [vmem] * (len(args) - smem),
        out_specs=[vmem] * len(shapes),
        compiler_params=pltpu.CompilerParams(vmem_limit_bytes=32 * 1024 * 1024),
    )(*args)


def on_device(
    cam_jac, point_jac, residuals, obs_camera, obs_point, obs_count, cam_damp, pt_damp, partner_mask
):
    n = cam_jac.shape[1]
    inner = n - 128
    groups = lax.axis_size("group")
    own = lax.axis_index("group").astype(jnp.int32)
    partner = jnp.stack([jnp.bitwise_xor(partner_mask[0], own), own])
    point_ids = obs_point[None]

    def over_dev(values, axis=1):
        return lax.all_to_all(values, "dev", split_axis=axis, concat_axis=axis, tiled=True)

    def over_group(values):
        return lax.all_to_all(values, "group", split_axis=0, concat_axis=0, tiled=True)

    field, fields, pair, back = (9, 128), (2, 9, 128), [(2, inner), (2, 128)], (3, inner)
    pay, outer, outer_sum, placed, inverse = call(
        setup_kernel, "setup", 1,
        [(inner // 128, 24, 128), (24, 128), (18, 128), (48, n), (48, 128)],
        obs_count, cam_jac, point_jac, residuals, obs_camera[None], point_ids, pt_damp,
    )
    pay = over_dev(pay, 0)
    (sums,) = call(
        start_sum_kernel, "start_sum", 0, [(groups, 36, 128)], pay, outer_sum, cam_damp
    )
    moved, outer_moved, remainder, precond, direction = call(
        start_kernel, "start", 1, pair + [fields] * 3,
        partner, over_group(sums), outer_sum, pay, outer,
    )
    points = (placed, point_ids, inverse, outer, cam_damp)
    kept, outer_sum = call(
        point_first_kernel, "point_first", 0, [back, field],
        over_dev(moved), outer_moved, *points, remainder, direction,
    )
    kept = over_dev(kept)
    (images,) = call(
        image_kernel, "image", 0, [(groups, 19, 128)], kept, outer_sum, pay, cam_damp, direction
    )
    moved, outer_moved, remainder, scaled, image, totals = call(
        camera_kernel, "camera", 1, pair + [fields] * 2 + [field, (1, 128)],
        partner, over_group(images), outer_sum, pay, outer, remainder, precond, direction,
    )
    kept, outer_sum = call(
        point_next_kernel, "point_next", 0, [back, field],
        over_dev(moved), outer_moved, *points, remainder, scaled, image,
    )
    kept = over_dev(kept)
    (images,) = call(pair_kernel, "pair", 0, [(groups, 10, 128)], kept, outer_sum)
    (next_image,) = call(inner_kernel, "inner", 0, [field], kept, pay, cam_damp, scaled)
    update, remainder = call(
        last_kernel, "last", 1, [field] * 2,
        partner, over_group(images), next_image, remainder, scaled, direction, image, totals,
    )
    return (update, remainder)


def solution(mesh):
    slots, rows = P(None, ("group", "dev")), P(("group", "dev"))
    return jax.shard_map(
        on_device,
        mesh=mesh,
        in_specs=(
            slots, slots, slots, rows, rows, P(("group", "dev"), None), slots, slots, P("dev"),
        ),
        out_specs=(slots, slots),
        check_vma=False,
    )
```

```python
import jax
import jax.numpy as jnp
from jax import lax
from jax.experimental import pallas as pl
from jax.experimental.pallas import tpu as pltpu
from jax.sharding import PartitionSpec as P

F32 = jnp.float32
BF16 = jnp.bfloat16
ROWS = 21
PAIRS = ((0, 0), (0, 1), (0, 2), (1, 1), (1, 2), (2, 2))


def one_hot(ids, count):
    rows = lax.broadcasted_iota(jnp.int32, (count, ids.shape[1]), 0)
    return jnp.where(rows == ids, 1.0, 0.0).astype(BF16)


def pieces(values, count):
    found = []
    for _ in range(count - 1):
        found.append(values.astype(BF16).astype(F32))
        values = values - found[-1]
    return found + [values]


def collect(values, chosen, count=2):
    m = values.shape[0]
    stacked = jnp.concatenate(pieces(values, count), 0).astype(BF16)
    sums = lax.dot_general(
        stacked, chosen, (((1,), (1,)), ((), ())), preferred_element_type=F32
    )
    total = sums[0:m]
    for i in range(1, count):
        total = total + sums[i * m : (i + 1) * m]
    return total


def fetch(items, chosen):
    stacked = jnp.concatenate(pieces(items, 2), 1).astype(BF16)
    return jnp.dot(
        stacked, jnp.concatenate([chosen, chosen], 0), preferred_element_type=F32
    )


def col_sum(values):
    return jnp.sum(values, axis=0, keepdims=True)


def total(values):
    return jnp.sum(values, keepdims=True)


def lane_blocks(row):
    out = row[:, 0:128]
    for b in range(1, row.shape[1] // 128):
        out = out + row[:, b * 128 : (b + 1) * 128]
    return out


def scalar_row(values):
    lanes = lax.broadcasted_iota(jnp.int32, (1, 128), 1)
    row = jnp.broadcast_to(values[0], (1, 128))
    for i in range(1, len(values)):
        row = jnp.where(lanes < 32 * i, row, values[i])
    return row


def scalars(row, count):
    return [row[:, 32 * i : 32 * i + 1] for i in range(count)]


def put_rows(ref, rows):
    for r, row in enumerate(rows):
        ref[r : r + 1, :] = row


def repeat(row, width):
    return jnp.concatenate([row] * (width // 128), 1)


def with_outer(in_ref, out_ref, r):
    return jnp.concatenate([in_ref[r : r + 1, :], out_ref[r : r + 1, :]], 1)


def solve_points(inverse, sums):
    c = [inverse[8 * i : 8 * i + 8] for i in range(6)]
    g = [sums[8 * i : 8 * i + 8] for i in range(3)]
    return jnp.concatenate(
        [
            c[0] * g[0] + c[1] * g[1] + c[2] * g[2],
            c[1] * g[0] + c[3] * g[1] + c[4] * g[2],
            c[2] * g[0] + c[4] * g[1] + c[5] * g[2],
        ],
        0,
    )


def spread_points(placed, first, second):
    return jnp.concatenate(
        [
            placed[8 * r : 8 * r + 8] * first + placed[24 + 8 * r : 32 + 8 * r] * second
            for r in range(3)
        ],
        0,
    )


def pull_points(placed, pulled, first, second):
    v0 = placed[0:8] * pulled[0:8] + placed[8:16] * pulled[8:16] + placed[16:24] * pulled[16:24]
    v1 = placed[24:32] * pulled[0:8] + placed[32:40] * pulled[8:16] + placed[40:48] * pulled[16:24]
    return first - col_sum(v0), second - col_sum(v1)


def setup_kernel(*refs):
    inputs, mask, outputs, copies, sems = refs[:7], refs[7], refs[8:15], refs[15:22], refs[22]
    copying = [
        pltpu.make_async_copy(source, copy, sems.at[i])
        for i, (source, copy) in enumerate(zip(inputs, copies))
    ]
    for copy in copying:
        copy.start()
    setup(copying, *copies, mask, *outputs)


def setup(
    copying, point_id_ref, count_ref, point_ref, res_ref, damp_ref, cam_ref, cam_id_ref, mask_ref,
    in_ref, outer_ref, outer_sum_ref, placed_ref, inverse_ref, ids_ref, partner_ref,
):
    n = cam_ref.shape[1]
    inner = n - 128
    lanes = lax.broadcasted_iota(jnp.int32, (1, 128), 1)
    copying[1].wait()
    live = jnp.concatenate(
        [jnp.where(lanes < count_ref[0, b], 1.0, 0.0) for b in range(n // 128)], 1
    )
    copying[0].wait()
    ids = point_id_ref[...].reshape(1, n)
    ids_ref[...] = ids
    chosen = one_hot(jnp.bitwise_and(ids, 127), 128)
    high = jnp.right_shift(ids, 7)
    digit = jnp.where(lax.broadcasted_iota(jnp.int32, (8, n), 0) == high, live, 0.0)
    copying[2].wait()
    for r in range(6):
        placed_ref[8 * r : 8 * r + 8, :] = digit * point_ref[r : r + 1, :]
    placed = placed_ref[...]
    part = [placed[8 * r : 8 * r + 8] for r in range(6)]
    copying[3].wait()
    first, second = res_ref[0:1, :], res_ref[1:2, :]
    squares = [part[a] * part[b] + part[3 + a] * part[3 + b] for a, b in PAIRS]
    blocks = collect(jnp.concatenate(squares, 0), chosen, 3)
    sums = collect(spread_points(placed, first, second), chosen)
    b = [blocks[8 * i : 8 * i + 8] for i in range(6)]
    copying[4].wait()
    for axis, entry in ((0, 0), (1, 3), (2, 5)):
        damp = damp_ref[axis : axis + 1, :]
        b[entry] = b[entry] + jnp.concatenate(
            [damp[:, 128 * h : 128 * h + 128] for h in range(8)], 0
        )
    cof = [
        b[3] * b[5] - b[4] * b[4],
        b[2] * b[4] - b[1] * b[5],
        b[1] * b[4] - b[2] * b[3],
        b[0] * b[5] - b[2] * b[2],
        b[1] * b[2] - b[0] * b[4],
        b[0] * b[3] - b[1] * b[1],
    ]
    det = b[0] * cof[0] + b[1] * cof[1] + b[2] * cof[2]
    inverse = jnp.concatenate([c / det for c in cof], 0)
    inverse_ref[...] = inverse
    pulled = fetch(solve_points(inverse, sums), chosen)
    first, second = pull_points(placed, pulled, first, second)
    copying[5].wait()
    copying[6].wait()
    partner_ref[0] = jnp.bitwise_xor(mask_ref[0], lax.axis_index("group"))
    partner_ref[1] = lax.axis_index("group")
    rows = cam_ref[...] * live
    cam_ids = cam_id_ref[...].reshape(1, n).astype(F32)

    every = jnp.concatenate([rows, first, second, cam_ids, jnp.zeros((3, n), F32)], 0)
    for i in range(inner // 128):
        in_ref[ROWS * i : ROWS * i + ROWS, :] = every[:ROWS, 128 * i : 128 * i + 128]
    outer = every[:, inner:]
    outer_ref[...] = outer
    outer_sum_ref[...] = start_sums(outer)


def spread_cams(owned, first, second):
    row = lax.broadcasted_iota(jnp.int32, owned.shape, 0)
    return owned * jnp.where(row < 9, first, jnp.where(row < 18, second, 0.0))


def halves(sums):
    return sums[0:9] + sums[9:18]


def apply_cams(owned, values, chosen):
    twice = jnp.concatenate([values, values, jnp.zeros((6, 128), F32)], 0)
    product = owned * fetch(twice, chosen)
    row = lax.broadcasted_iota(jnp.int32, (8, owned.shape[1]), 0)
    middle = product[8:16]
    first = col_sum(product[0:8] + jnp.where(row == 0, middle, 0.0))
    second = col_sum(product[16:24] + jnp.where(row == 0, 0.0, middle))
    return first, second


def ids_of(owned):
    return one_hot(owned[20:21].astype(jnp.int32), 128)


def start_sums(owned):
    row = lax.broadcasted_iota(jnp.int32, owned.shape, 0)
    squares = jnp.where(row < 18, owned * owned, 0.0)
    terms = jnp.concatenate([spread_cams(owned, owned[18:19], owned[19:20]), squares], 0)
    sums = collect(terms, ids_of(owned))
    return jnp.concatenate([halves(sums[0:24]), halves(sums[24:48])], 0)


def blocks_of(pay_ref):
    rows = [pay_ref[i : i + ROWS, :] for i in range(0, pay_ref.shape[0], ROWS)]
    owned = jnp.concatenate(rows, 1)
    return jnp.concatenate([owned, jnp.zeros((24 - ROWS, owned.shape[1]), F32)], 0)


def start_sum_kernel(pay_ref, outer_sum_ref, damp_ref, group_ref):
    sums = start_sums(blocks_of(pay_ref))
    for i in range(group_ref.shape[0]):
        group_ref[i, 0:9, :] = sums[0:9]
        group_ref[i, 9:18, :] = sums[9:18] + damp_ref[...]
        group_ref[i, 18:36, :] = outer_sum_ref[...]


def put_moved(in_ref, out_ref, pay_ref, outer_ref, own, twin):
    owned = blocks_of(pay_ref)
    put_rows(in_ref, apply_cams(owned, own, ids_of(owned)))
    outer = outer_ref[...]
    put_rows(out_ref, apply_cams(outer, twin, ids_of(outer)))


def start_kernel(
    partner_ref, group_ref, outer_sum_ref, pay_ref, outer_ref,
    in_ref, out_ref, rem_ref, pre_ref, dir_ref,
):
    theirs = group_ref[partner_ref[0]]
    mine = group_ref[partner_ref[1]]
    sums = [mine[0:18] + theirs[18:36], theirs[0:18] + outer_sum_ref[...]]
    for i in range(2):
        remainder = -sums[i][0:9]
        precond = 1.0 / sums[i][9:18]
        rem_ref[i] = remainder
        pre_ref[i] = precond
        dir_ref[i] = precond * remainder
    put_moved(in_ref, out_ref, pay_ref, outer_ref, dir_ref[0], dir_ref[1])


def point_side(in_ref, out_ref, placed_ref, point_id_ref, inverse_ref):
    placed = placed_ref[...]
    first, second = with_outer(in_ref, out_ref, 0), with_outer(in_ref, out_ref, 1)
    chosen = one_hot(jnp.bitwise_and(point_id_ref[...], 127), 128)
    sums = collect(spread_points(placed, first, second), chosen)
    pulled = fetch(solve_points(inverse_ref[...], sums), chosen)
    kept = pull_points(placed, pulled, first, second)
    return kept, total(lane_blocks(first * kept[0] + second * kept[1]))


def put_kept(back_ref, outer_sum_ref, outer_ref, kept, values):
    inner = kept[0].shape[1] - 128
    row = scalar_row(values)
    for i in range(inner // 128):
        lo, hi = 128 * i, 128 * i + 128
        put_rows(back_ref.at[3 * i : 3 * i + 3], [kept[0][:, lo:hi], kept[1][:, lo:hi], row])
    outer = outer_ref[...]
    spread = spread_cams(outer, kept[0][:, inner:], kept[1][:, inner:])
    outer_sum_ref[...] = halves(collect(spread, ids_of(outer)))


def point_first_kernel(
    in_ref, out_ref, placed_ref, point_id_ref, inverse_ref, outer_ref, damp_ref, rem_ref, dir_ref,
    back_ref, outer_sum_ref,
):
    kept, bend = point_side(in_ref, out_ref, placed_ref, point_id_ref, inverse_ref)
    direction = dir_ref[0]
    bend = bend + total(damp_ref[...] * direction * direction)
    put_kept(back_ref, outer_sum_ref, outer_ref, kept, [total(rem_ref[0] * direction), bend])


def point_next_kernel(
    in_ref, out_ref, placed_ref, point_id_ref, inverse_ref, outer_ref, damp_ref,
    rem_ref, scaled_ref, image_ref,
    back_ref, outer_sum_ref,
):
    kept, bend = point_side(in_ref, out_ref, placed_ref, point_id_ref, inverse_ref)
    scaled = scaled_ref[0]
    bend = bend + total(damp_ref[...] * scaled * scaled)
    values = [total(rem_ref[0] * scaled), bend, total(image_ref[...] * scaled)]
    put_kept(back_ref, outer_sum_ref, outer_ref, kept, values)


def back_row(back_ref, r):
    return jnp.concatenate([back_ref[i : i + 1, :] for i in range(r, back_ref.shape[0], 3)], 1)


def inner_image(back_ref, pay_ref, damp_ref, field):
    owned = blocks_of(pay_ref)
    spread = spread_cams(owned, back_row(back_ref, 0), back_row(back_ref, 1))
    return damp_ref[...] * field + halves(collect(spread, ids_of(owned)))


def image_kernel(back_ref, outer_sum_ref, pay_ref, damp_ref, dir_ref, group_ref):
    image = inner_image(back_ref, pay_ref, damp_ref, dir_ref[0])
    partial = lane_blocks(back_row(back_ref, 2))
    for i in range(group_ref.shape[0]):
        group_ref[i, 0:9, :] = image
        group_ref[i, 9:18, :] = outer_sum_ref[...]
        group_ref[i, 18:19, :] = partial


def group_total(group_ref, r):
    row = group_ref[0, r : r + 1, :]
    for i in range(1, group_ref.shape[0]):
        row = row + group_ref[i, r : r + 1, :]
    return row


def camera_kernel(
    partner_ref, group_ref, outer_sum_ref, pay_ref, outer_ref, rem_ref, pre_ref, dir_ref,
    in_ref, out_ref, next_rem_ref, scaled_ref, image_ref, sums_ref,
):
    sums = group_total(group_ref, 18)
    sums_ref[...] = sums
    norm, bend = scalars(sums, 2)
    step = norm / bend
    theirs = group_ref[partner_ref[0]]
    mine = group_ref[partner_ref[1]]
    images = [mine[0:9] + theirs[9:18], theirs[0:9] + outer_sum_ref[...]]
    image_ref[...] = images[0]
    for i in range(2):
        remainder = rem_ref[i] - step * images[i]
        next_rem_ref[i] = remainder
        scaled_ref[i] = pre_ref[i] * remainder
    put_moved(in_ref, out_ref, pay_ref, outer_ref, scaled_ref[0], scaled_ref[1])


def pair_kernel(back_ref, outer_sum_ref, pay_ref, damp_ref, scaled_ref, group_ref, image_ref):
    image_ref[...] = inner_image(back_ref, pay_ref, damp_ref, scaled_ref[0])
    partial = lane_blocks(back_row(back_ref, 2))
    for i in range(group_ref.shape[0]):
        group_ref[i, 0:9, :] = outer_sum_ref[...]
        group_ref[i, 9:10, :] = partial


def last_kernel(
    partner_ref, group_ref, inner_ref, rem_ref, scaled_ref, dir_ref, image_ref, sums_ref,
    update_ref, next_rem_ref,
):
    norm, bend = scalars(sums_ref[...], 2)
    next_norm, next_bend, cross = scalars(group_total(group_ref, 9), 3)
    ratio = next_norm / norm
    next_bend = next_bend + ratio * (2.0 * cross + ratio * bend)
    step = next_norm / next_bend
    image = inner_ref[...] + group_ref[partner_ref[0], 0:9, :] + ratio * image_ref[...]
    direction = dir_ref[0]
    update_ref[...] = norm / bend * direction + step * (scaled_ref[0] + ratio * direction)
    next_rem_ref[...] = rem_ref[0] - step * image


def call(kernel, name, smem, shapes, *args):
    vmem = pl.BlockSpec(memory_space=pltpu.VMEM)
    scalar = pl.BlockSpec(memory_space=pltpu.SMEM)
    return pl.pallas_call(
        kernel,
        name=name,
        out_shape=[jax.ShapeDtypeStruct(shape, F32) for shape in shapes],
        in_specs=[scalar] * smem + [vmem] * (len(args) - smem),
        out_specs=[vmem] * len(shapes),
        compiler_params=pltpu.CompilerParams(vmem_limit_bytes=32 * 1024 * 1024),
    )(*args)


def start(*args):
    n = args[0].shape[0]
    shapes = [(ROWS * (n // 128 - 1), 128), (24, 128), (18, 128), (48, n), (48, 128), (1, n), (2,)]
    kinds = [F32] * 5 + [jnp.int32] * 2
    copies = [
        pltpu.SMEM(a.shape, a.dtype) if i == 1 else pltpu.VMEM(a.shape, a.dtype)
        for i, a in enumerate(args[:-1])
    ]
    args = [pltpu.with_memory_space_constraint(a, pltpu.HBM) for a in args[:-1]] + [args[-1]]
    return pl.pallas_call(
        setup_kernel,
        name="setup",
        out_shape=[jax.ShapeDtypeStruct(s, k) for s, k in zip(shapes, kinds)],
        in_specs=[pl.BlockSpec(memory_space=pltpu.HBM)] * len(copies)
        + [pl.BlockSpec(memory_space=pltpu.SMEM)],
        out_specs=[pl.BlockSpec(memory_space=pltpu.VMEM)] * 6
        + [pl.BlockSpec(memory_space=pltpu.SMEM)],
        scratch_shapes=copies + [pltpu.SemaphoreType.DMA((len(copies),))],
        compiler_params=pltpu.CompilerParams(vmem_limit_bytes=32 * 1024 * 1024),
    )(*args)


def on_device(
    cam_jac, point_jac, residuals, obs_camera, obs_point, obs_count, cam_damp, pt_damp, partner_mask
):
    n = cam_jac.shape[1]
    inner = n - 128
    groups = lax.axis_size("group")

    def over_dev(values):
        return lax.all_to_all(values, "dev", split_axis=1, concat_axis=1, tiled=True)

    def rows_over_dev(values):
        blocks = values.reshape(inner // 128, -1, 1, 128)
        got = lax.all_to_all(blocks, "dev", split_axis=0, concat_axis=0, tiled=True)
        return got.reshape(values.shape)

    def over_group(values):
        return lax.all_to_all(values, "group", split_axis=0, concat_axis=0, tiled=True)

    field, fields, pair, back = (9, 128), (2, 9, 128), [(2, inner), (2, 128)], (inner // 128 * 3, 128)
    pay, outer, outer_sum, placed, inverse, point_ids, partner = start(
        obs_point, obs_count, point_jac, residuals, pt_damp, cam_jac, obs_camera, partner_mask
    )
    pay = rows_over_dev(pay)
    (sums,) = call(
        start_sum_kernel, "start_sum", 0, [(groups, 36, 128)], pay, outer_sum, cam_damp
    )
    moved, outer_moved, remainder, precond, direction = call(
        start_kernel, "start", 1, pair + [fields] * 3,
        partner, over_group(sums), outer_sum, pay, outer,
    )
    points = (placed, point_ids, inverse, outer, cam_damp)
    kept, outer_sum = call(
        point_first_kernel, "point_first", 0, [back, field],
        over_dev(moved), outer_moved, *points, remainder, direction,
    )
    kept = rows_over_dev(kept)
    (images,) = call(
        image_kernel, "image", 0, [(groups, 19, 128)], kept, outer_sum, pay, cam_damp, direction
    )
    moved, outer_moved, remainder, scaled, image, totals = call(
        camera_kernel, "camera", 1, pair + [fields] * 2 + [field, (1, 128)],
        partner, over_group(images), outer_sum, pay, outer, remainder, precond, direction,
    )
    kept, outer_sum = call(
        point_next_kernel, "point_next", 0, [back, field],
        over_dev(moved), outer_moved, *points, remainder, scaled, image,
    )
    kept = rows_over_dev(kept)
    images, next_image = call(
        pair_kernel, "pair", 0, [(groups, 10, 128), field], kept, outer_sum, pay, cam_damp, scaled
    )
    update, remainder = call(
        last_kernel, "last", 1, [field] * 2,
        partner, over_group(images), next_image, remainder, scaled, direction, image, totals,
    )
    return (update, remainder)


def solution(mesh):
    slots, rows = P(None, ("group", "dev")), P(("group", "dev"))
    return jax.shard_map(
        on_device,
        mesh=mesh,
        in_specs=(
            slots, slots, slots, rows, rows, P(("group", "dev"), None), slots, slots, P("dev"),
        ),
        out_specs=(slots, slots),
        check_vma=False,
    )
```

```python
import jax
import jax.numpy as jnp
from jax import lax
from jax.experimental import pallas as pl
from jax.experimental.pallas import tpu as pltpu
from jax.sharding import PartitionSpec as P

F32 = jnp.float32
BF16 = jnp.bfloat16
STEP = 512
ROWS = 21
PAIRS = ((0, 0), (0, 1), (0, 2), (1, 1), (1, 2), (2, 2))


def one_hot(ids, count):
    rows = lax.broadcasted_iota(jnp.int32, (count, ids.shape[1]), 0)
    return jnp.where(rows == ids, 1.0, 0.0).astype(BF16)


def pieces(values, count):
    found = []
    for _ in range(count - 1):
        found.append(values.astype(BF16).astype(F32))
        values = values - found[-1]
    return jnp.concatenate(found + [values], 0).astype(BF16)


def unstack(sums, count):
    m = sums.shape[0] // count
    total = sums[0:m]
    for i in range(1, count):
        total = total + sums[i * m : (i + 1) * m]
    return total


def collect(values, chosen_t, count=2):
    return jnp.dot(pieces(values, count), chosen_t, preferred_element_type=F32)


def fetch(stacked, chosen):
    return unstack(jnp.dot(stacked, chosen, preferred_element_type=F32), 2)


def col_sum(values):
    return jnp.sum(values, axis=0, keepdims=True)


def total(values):
    return jnp.sum(values, keepdims=True)


def lane_blocks(row):
    out = row[:, 0:128]
    for b in range(1, row.shape[1] // 128):
        out = out + row[:, b * 128 : (b + 1) * 128]
    return out


def spans(n):
    return [(lo, min(lo + STEP, n)) for lo in range(0, n, STEP)]


def added(sums, more):
    return more if sums is None else sums + more


def scalar_row(values):
    lanes = lax.broadcasted_iota(jnp.int32, (1, 128), 1)
    row = jnp.broadcast_to(values[0], (1, 128))
    for i in range(1, len(values)):
        row = jnp.where(lanes < 32 * i, row, values[i])
    return row


def scalars(row, count):
    return [row[:, 32 * i : 32 * i + 1] for i in range(count)]


def put_rows(ref, rows):
    for r, row in enumerate(rows):
        ref[r : r + 1, :] = row


def solve_points(inverse, sums):
    c = [inverse[8 * i : 8 * i + 8] for i in range(6)]
    g = [sums[8 * i : 8 * i + 8] for i in range(3)]
    return jnp.concatenate(
        [
            c[0] * g[0] + c[1] * g[1] + c[2] * g[2],
            c[1] * g[0] + c[3] * g[1] + c[4] * g[2],
            c[2] * g[0] + c[4] * g[1] + c[5] * g[2],
        ],
        0,
    )


def slots_of(in_ref, out_ref, r, lo, hi):
    inner = in_ref.shape[1]
    if hi <= inner:
        return in_ref[r : r + 1, lo:hi]
    if lo >= inner:
        return out_ref[r : r + 1, lo - inner : hi - inner]
    return jnp.concatenate([in_ref[r : r + 1, lo:inner], out_ref[r : r + 1, : hi - inner]], 1)


def spread_points(placed_ref, first, second, lo, hi):
    return jnp.concatenate(
        [
            placed_ref[8 * r : 8 * r + 8, lo:hi] * first
            + placed_ref[24 + 8 * r : 32 + 8 * r, lo:hi] * second
            for r in range(3)
        ],
        0,
    )


def pull_points(placed_ref, pulled, first, second, lo, hi):
    def image(base):
        out = placed_ref[base : base + 8, lo:hi] * pulled[0:8]
        out = out + placed_ref[base + 8 : base + 16, lo:hi] * pulled[8:16]
        return col_sum(out + placed_ref[base + 16 : base + 24, lo:hi] * pulled[16:24])

    return first - image(0), second - image(24)


def setup_kernel(*refs):
    inputs, mask, outputs, copies, sems = refs[:7], refs[7], refs[8:18], refs[18:25], refs[25]
    copying = [
        pltpu.make_async_copy(source, copy, sems.at[i])
        for i, (source, copy) in enumerate(zip(inputs, copies))
    ]
    for copy in copying:
        copy.start()
    setup(copying, *copies, mask, *outputs)


def setup(
    copying, point_id_ref, count_ref, point_ref, res_ref, damp_ref, cam_ref, cam_id_ref, mask_ref,
    in_ref, outer_ref, outer_chosen_ref, outer_chosen_t_ref, outer_sum_ref, placed_ref,
    inverse_ref, chosen_ref, chosen_t_ref, partner_ref,
):
    n = cam_ref.shape[1]
    inner = n - 128
    partner = jnp.bitwise_xor(mask_ref[0], lax.axis_index("group"))
    partner_ref[...] = jnp.broadcast_to(partner, (1, 128)).astype(jnp.int32)
    copying[0].wait()
    ids = point_id_ref[...].reshape(1, n)
    low, high = jnp.bitwise_and(ids, 127), jnp.right_shift(ids, 7)
    for lo, hi in spans(n):
        chosen = one_hot(low[:, lo:hi], 128)
        chosen_ref[:, lo:hi] = chosen
        chosen_t_ref[lo:hi, :] = chosen.T
    lanes = lax.broadcasted_iota(jnp.int32, (1, 128), 1)
    copying[1].wait()
    live = jnp.concatenate(
        [jnp.where(lanes < count_ref[0, b], 1.0, 0.0) for b in range(n // 128)], 1
    )
    copying[2].wait()
    copying[3].wait()
    sums = None
    for lo, hi in spans(n):
        digit = lax.broadcasted_iota(jnp.int32, (8, hi - lo), 0)
        digit = jnp.where(digit == high[:, lo:hi], live[:, lo:hi], 0.0)
        for r in range(6):
            placed_ref[8 * r : 8 * r + 8, lo:hi] = digit * point_ref[r : r + 1, lo:hi]
        part = [placed_ref[8 * r : 8 * r + 8, lo:hi] for r in range(6)]
        terms = [part[a] * part[b] + part[3 + a] * part[3 + b] for a, b in PAIRS]
        terms.append(
            spread_points(placed_ref, res_ref[0:1, lo:hi], res_ref[1:2, lo:hi], lo, hi)
        )
        sums = added(sums, collect(jnp.concatenate(terms, 0), chosen_t_ref[lo:hi, :], 3))
    sums = unstack(sums, 3)
    b = [sums[8 * i : 8 * i + 8] for i in range(6)]
    copying[4].wait()
    for axis, entry in ((0, 0), (1, 3), (2, 5)):
        damp = damp_ref[axis : axis + 1, :]
        b[entry] = b[entry] + jnp.concatenate(
            [damp[:, 128 * h : 128 * h + 128] for h in range(8)], 0
        )
    cof = [
        b[3] * b[5] - b[4] * b[4],
        b[2] * b[4] - b[1] * b[5],
        b[1] * b[4] - b[2] * b[3],
        b[0] * b[5] - b[2] * b[2],
        b[1] * b[2] - b[0] * b[4],
        b[0] * b[3] - b[1] * b[1],
    ]
    det = b[0] * cof[0] + b[1] * cof[1] + b[2] * cof[2]
    inverse = jnp.concatenate([c / det for c in cof], 0)
    inverse_ref[...] = inverse
    stacked = pieces(solve_points(inverse, sums[48:72]), 2)
    copying[5].wait()
    copying[6].wait()
    cam_ids = cam_id_ref[...].reshape(1, n).astype(F32)
    for lo, hi in spans(n):
        pulled = fetch(stacked, chosen_ref[:, lo:hi])
        first, second = pull_points(
            placed_ref, pulled, res_ref[0:1, lo:hi], res_ref[1:2, lo:hi], lo, hi
        )
        rows = cam_ref[:, lo:hi] * live[:, lo:hi]
        every = jnp.concatenate(
            [rows, first, second, cam_ids[:, lo:hi], jnp.zeros((3, hi - lo), F32)], 0
        )
        for at in range(lo, hi, 128):
            block = every[:, at - lo : at - lo + 128]
            if at < inner:
                i = at // 128
                in_ref[ROWS * i : ROWS * i + ROWS, :] = block[:ROWS]
            else:
                outer_ref[...] = block
                outer_chosen = ids_of(block)
                outer_chosen_ref[...] = outer_chosen
                outer_chosen_t_ref[...] = outer_chosen.T
                outer_sum_ref[...] = both_halves(start_terms(block, outer_chosen.T))


def ids_of(owned):
    return one_hot(owned[20:21].astype(jnp.int32), 128)


def spread_cams(owned, first, second):
    row = lax.broadcasted_iota(jnp.int32, owned.shape, 0)
    return owned * jnp.where(row < 9, first, jnp.where(row < 18, second, 0.0))


def halves(sums):
    return sums[0:9] + sums[9:18]


def start_terms(owned, chosen_t):
    row = lax.broadcasted_iota(jnp.int32, owned.shape, 0)
    squares = jnp.where(row < 18, owned * owned, 0.0)
    terms = jnp.concatenate([spread_cams(owned, owned[18:19], owned[19:20]), squares], 0)
    return collect(terms, chosen_t)


def both_halves(sums):
    sums = unstack(sums, 2)
    return jnp.concatenate([halves(sums[0:24]), halves(sums[24:48])], 0)


def inner_of(pay_ref):
    return pay_ref.shape[0] // ROWS * 128


def owned_of(pay_ref, lo, hi):
    rows = [pay_ref[ROWS * i : ROWS * i + ROWS, :] for i in range(lo // 128, hi // 128)]
    return jnp.concatenate([jnp.concatenate(rows, 1), jnp.zeros((24 - ROWS, hi - lo), F32)], 0)


def start_sum_kernel(pay_ref, outer_sum_ref, damp_ref, group_ref, chosen_ref, chosen_t_ref):
    sums = None
    for lo, hi in spans(inner_of(pay_ref)):
        owned = owned_of(pay_ref, lo, hi)
        chosen = ids_of(owned)
        chosen_ref[:, lo:hi] = chosen
        chosen_t = chosen.T
        chosen_t_ref[lo:hi, :] = chosen_t
        sums = added(sums, start_terms(owned, chosen_t))
    sums = both_halves(sums)
    for i in range(group_ref.shape[0]):
        group_ref[i, 0:9, :] = sums[0:9]
        group_ref[i, 9:18, :] = sums[9:18] + damp_ref[...]
        group_ref[i, 18:36, :] = outer_sum_ref[...]


def twice(values):
    return pieces(jnp.concatenate([values, values, jnp.zeros((6, 128), F32)], 0), 2)


def apply_cams(owned, stacked, chosen):
    product = owned * fetch(stacked, chosen)
    row = lax.broadcasted_iota(jnp.int32, (8, owned.shape[1]), 0)
    middle = product[8:16]
    first = col_sum(product[0:8] + jnp.where(row == 0, middle, 0.0))
    second = col_sum(product[16:24] + jnp.where(row == 0, 0.0, middle))
    return first, second


def put_moved(in_ref, out_ref, pay_ref, chosen_ref, outer_ref, outer_chosen_ref, own, twin):
    stacked = twice(own)
    for lo, hi in spans(inner_of(pay_ref)):
        moved = apply_cams(owned_of(pay_ref, lo, hi), stacked, chosen_ref[:, lo:hi])
        in_ref[0:1, lo:hi], in_ref[1:2, lo:hi] = moved
    put_rows(out_ref, apply_cams(outer_ref[...], twice(twin), outer_chosen_ref[...]))


def partner_block(partner_ref, group_ref, lo, hi):
    partner = partner_ref[...]
    out = group_ref[0, lo:hi, :]
    for i in range(1, group_ref.shape[0]):
        out = jnp.where(partner == i, group_ref[i, lo:hi, :], out)
    return out


def start_kernel(
    partner_ref, group_ref, sent_ref, outer_sum_ref, pay_ref, chosen_ref, outer_ref,
    outer_chosen_ref,
    in_ref, out_ref, rem_ref, pre_ref, dir_ref,
):
    theirs = partner_block(partner_ref, group_ref, 0, 36)
    sums = [sent_ref[0, 0:18, :] + theirs[18:36], theirs[0:18] + outer_sum_ref[...]]
    for i in range(2):
        remainder = -sums[i][0:9]
        precond = 1.0 / sums[i][9:18]
        rem_ref[i] = remainder
        pre_ref[i] = precond
        dir_ref[i] = precond * remainder
    put_moved(
        in_ref, out_ref, pay_ref, chosen_ref, outer_ref, outer_chosen_ref, dir_ref[0], dir_ref[1]
    )


def point_side(
    in_ref, out_ref, placed_ref, chosen_ref, chosen_t_ref, inverse_ref, outer_ref,
    outer_chosen_t_ref, back_ref, outer_sum_ref, values,
):
    n = placed_ref.shape[1]
    inner = n - 128
    sums = None
    for lo, hi in spans(n):
        first, second = slots_of(in_ref, out_ref, 0, lo, hi), slots_of(in_ref, out_ref, 1, lo, hi)
        terms = spread_points(placed_ref, first, second, lo, hi)
        sums = added(sums, collect(terms, chosen_t_ref[lo:hi, :]))
    stacked = pieces(solve_points(inverse_ref[...], unstack(sums, 2)), 2)
    bend = None
    for lo, hi in spans(n):
        first, second = slots_of(in_ref, out_ref, 0, lo, hi), slots_of(in_ref, out_ref, 1, lo, hi)
        pulled = fetch(stacked, chosen_ref[:, lo:hi])
        kept = pull_points(placed_ref, pulled, first, second, lo, hi)
        bend = added(bend, lane_blocks(first * kept[0] + second * kept[1]))
        for at in range(lo, hi, 128):
            rows = [k[:, at - lo : at - lo + 128] for k in kept]
            if at < inner:
                i = 3 * (at // 128)
                back_ref[i : i + 1, :], back_ref[i + 1 : i + 2, :] = rows
            else:
                spread = spread_cams(outer_ref[...], *rows)
                outer = collect(spread, outer_chosen_t_ref[...])
                outer_sum_ref[...] = halves(unstack(outer, 2))
    values[1] = values[1] + total(bend)
    row = scalar_row(values)
    for i in range(inner // 128):
        back_ref[3 * i + 2 : 3 * i + 3, :] = row


def point_first_kernel(
    in_ref, out_ref, placed_ref, chosen_ref, chosen_t_ref, inverse_ref, outer_ref,
    outer_chosen_t_ref, damp_ref,
    rem_ref, dir_ref,
    back_ref, outer_sum_ref,
):
    direction = dir_ref[0]
    values = [total(rem_ref[0] * direction), total(damp_ref[...] * direction * direction)]
    point_side(
        in_ref, out_ref, placed_ref, chosen_ref, chosen_t_ref, inverse_ref, outer_ref,
        outer_chosen_t_ref, back_ref, outer_sum_ref, values,
    )


def point_next_kernel(
    in_ref, out_ref, placed_ref, chosen_ref, chosen_t_ref, inverse_ref, outer_ref,
    outer_chosen_t_ref, damp_ref,
    rem_ref, scaled_ref, image_ref,
    back_ref, outer_sum_ref,
):
    scaled = scaled_ref[0]
    values = [
        total(rem_ref[0] * scaled),
        total(damp_ref[...] * scaled * scaled),
        total(image_ref[...] * scaled),
    ]
    point_side(
        in_ref, out_ref, placed_ref, chosen_ref, chosen_t_ref, inverse_ref, outer_ref,
        outer_chosen_t_ref, back_ref, outer_sum_ref, values,
    )


def back_row(back_ref, r, lo, hi):
    rows = [back_ref[3 * i + r : 3 * i + r + 1, :] for i in range(lo // 128, hi // 128)]
    return jnp.concatenate(rows, 1)


def inner_image(back_ref, pay_ref, chosen_t_ref, damp_ref, field):
    sums = None
    row = None
    for lo, hi in spans(inner_of(pay_ref)):
        first, second = back_row(back_ref, 0, lo, hi), back_row(back_ref, 1, lo, hi)
        spread = spread_cams(owned_of(pay_ref, lo, hi), first, second)
        sums = added(sums, collect(spread, chosen_t_ref[lo:hi, :]))
        row = added(row, lane_blocks(back_row(back_ref, 2, lo, hi)))
    return damp_ref[...] * field + halves(unstack(sums, 2)), row


def image_kernel(back_ref, outer_sum_ref, pay_ref, chosen_t_ref, damp_ref, dir_ref, group_ref):
    image, partial = inner_image(back_ref, pay_ref, chosen_t_ref, damp_ref, dir_ref[0])
    for i in range(group_ref.shape[0]):
        group_ref[i, 0:9, :] = image
        group_ref[i, 9:18, :] = outer_sum_ref[...]
        group_ref[i, 18:19, :] = partial


def group_total(group_ref, r):
    row = group_ref[0, r : r + 1, :]
    for i in range(1, group_ref.shape[0]):
        row = row + group_ref[i, r : r + 1, :]
    return row


def camera_kernel(
    partner_ref, group_ref, sent_ref, outer_sum_ref, pay_ref, chosen_ref, outer_ref,
    outer_chosen_ref, rem_ref, pre_ref, dir_ref,
    in_ref, out_ref, next_rem_ref, scaled_ref, image_ref, sums_ref,
):
    sums = group_total(group_ref, 18)
    sums_ref[...] = sums
    norm, bend = scalars(sums, 2)
    step = norm / bend
    theirs = partner_block(partner_ref, group_ref, 0, 18)
    images = [sent_ref[0, 0:9, :] + theirs[9:18], theirs[0:9] + outer_sum_ref[...]]
    image_ref[...] = images[0]
    for i in range(2):
        remainder = rem_ref[i] - step * images[i]
        next_rem_ref[i] = remainder
        scaled_ref[i] = pre_ref[i] * remainder
    put_moved(
        in_ref, out_ref, pay_ref, chosen_ref, outer_ref, outer_chosen_ref,
        scaled_ref[0], scaled_ref[1],
    )


def pair_kernel(
    back_ref, outer_sum_ref, pay_ref, chosen_t_ref, damp_ref, scaled_ref, group_ref, image_ref
):
    image, partial = inner_image(back_ref, pay_ref, chosen_t_ref, damp_ref, scaled_ref[0])
    image_ref[...] = image
    for i in range(group_ref.shape[0]):
        group_ref[i, 0:9, :] = outer_sum_ref[...]
        group_ref[i, 9:10, :] = partial


def last_kernel(
    partner_ref, group_ref, inner_ref, rem_ref, scaled_ref, dir_ref, image_ref, sums_ref,
    update_ref, next_rem_ref,
):
    norm, bend = scalars(sums_ref[...], 2)
    next_norm, next_bend, cross = scalars(group_total(group_ref, 9), 3)
    ratio = next_norm / norm
    next_bend = next_bend + ratio * (2.0 * cross + ratio * bend)
    step = next_norm / next_bend
    theirs = partner_block(partner_ref, group_ref, 0, 9)
    image = inner_ref[...] + theirs + ratio * image_ref[...]
    direction = dir_ref[0]
    update_ref[...] = norm / bend * direction + step * (scaled_ref[0] + ratio * direction)
    next_rem_ref[...] = rem_ref[0] - step * image


def call(kernel, name, shapes, *args):
    vmem = pl.BlockSpec(memory_space=pltpu.VMEM)
    return pl.pallas_call(
        kernel,
        name=name,
        out_shape=[jax.ShapeDtypeStruct(*shape) for shape in shapes],
        in_specs=[vmem] * len(args),
        out_specs=[vmem] * len(shapes),
        compiler_params=pltpu.CompilerParams(vmem_limit_bytes=32 * 1024 * 1024),
    )(*args)


def start(*args):
    n = args[0].shape[0]
    shapes = [
        ((ROWS * (n // 128 - 1), 128), F32),
        ((24, 128), F32),
        ((128, 128), BF16),
        ((128, 128), BF16),
        ((18, 128), F32),
        ((48, n), F32),
        ((48, 128), F32),
        ((128, n), BF16),
        ((n, 128), BF16),
        ((1, 128), jnp.int32),
    ]
    copies = [
        pltpu.SMEM(a.shape, a.dtype) if i == 1 else pltpu.VMEM(a.shape, a.dtype)
        for i, a in enumerate(args[:-1])
    ]
    args = [pltpu.with_memory_space_constraint(a, pltpu.HBM) for a in args[:-1]] + [args[-1]]
    return pl.pallas_call(
        setup_kernel,
        name="setup",
        out_shape=[jax.ShapeDtypeStruct(*shape) for shape in shapes],
        in_specs=[pl.BlockSpec(memory_space=pltpu.HBM)] * len(copies)
        + [pl.BlockSpec(memory_space=pltpu.SMEM)],
        out_specs=[pl.BlockSpec(memory_space=pltpu.VMEM)] * len(shapes),
        scratch_shapes=copies + [pltpu.SemaphoreType.DMA((len(copies),))],
        compiler_params=pltpu.CompilerParams(vmem_limit_bytes=32 * 1024 * 1024),
    )(*args)


def on_device(
    cam_jac, point_jac, residuals, obs_camera, obs_point, obs_count, cam_damp, pt_damp, partner_mask
):
    n = cam_jac.shape[1]
    inner = n - 128
    groups = lax.axis_size("group")

    def over_dev(values):
        return lax.all_to_all(values, "dev", split_axis=1, concat_axis=1, tiled=True)

    def rows_over_dev(values):
        blocks = values.reshape(inner // 128, -1, 1, 128)
        got = lax.all_to_all(blocks, "dev", split_axis=0, concat_axis=0, tiled=True)
        return got.reshape(values.shape)

    def over_group(values):
        return lax.all_to_all(values, "group", split_axis=0, concat_axis=0, tiled=True)

    def sends(rows):
        return ((groups, rows, 128), F32)

    field, fields, line = ((9, 128), F32), ((2, 9, 128), F32), ((1, 128), F32)
    pair, back = [((2, inner), F32), ((2, 128), F32)], ((inner // 128 * 3, 128), F32)
    pay, outer, outer_chosen, outer_chosen_t, outer_sum, placed, inverse, *ones, partner = start(
        obs_point, obs_count, point_jac, residuals, pt_damp, cam_jac, obs_camera, partner_mask
    )
    pay = rows_over_dev(pay)
    sums, chosen, chosen_t = call(
        start_sum_kernel, "start_sum", [sends(36), ((128, inner), BF16), ((inner, 128), BF16)],
        pay, outer_sum, cam_damp,
    )
    cameras = (pay, chosen, outer, outer_chosen)
    moved, outer_moved, remainder, precond, direction = call(
        start_kernel, "start", pair + [fields] * 3,
        partner, over_group(sums), sums, outer_sum, *cameras,
    )
    points = (placed, *ones, inverse, outer, outer_chosen_t, cam_damp)
    kept, outer_sum = call(
        point_first_kernel, "point_first", [back, field],
        over_dev(moved), outer_moved, *points, remainder, direction,
    )
    kept = rows_over_dev(kept)
    (images,) = call(
        image_kernel, "image", [sends(19)], kept, outer_sum, pay, chosen_t, cam_damp, direction
    )
    moved, outer_moved, remainder, scaled, image, totals = call(
        camera_kernel, "camera", pair + [fields] * 2 + [field, line],
        partner, over_group(images), images, outer_sum, *cameras, remainder, precond, direction,
    )
    kept, outer_sum = call(
        point_next_kernel, "point_next", [back, field],
        over_dev(moved), outer_moved, *points, remainder, scaled, image,
    )
    kept = rows_over_dev(kept)
    images, next_image = call(
        pair_kernel, "pair", [sends(10), field], kept, outer_sum, pay, chosen_t, cam_damp, scaled
    )
    update, remainder = call(
        last_kernel, "last", [field] * 2,
        partner, over_group(images), next_image, remainder, scaled, direction, image, totals,
    )
    return (update, remainder)


def solution(mesh):
    slots, rows = P(None, ("group", "dev")), P(("group", "dev"))
    return jax.shard_map(
        on_device,
        mesh=mesh,
        in_specs=(
            slots, slots, slots, rows, rows, P(("group", "dev"), None), slots, slots, P("dev"),
        ),
        out_specs=(slots, slots),
        check_vma=False,
    )
```

```python
import jax
import jax.numpy as jnp
from jax import lax
from jax.experimental import pallas as pl
from jax.experimental.pallas import tpu as pltpu
from jax.sharding import PartitionSpec as P

F32 = jnp.float32
BF16 = jnp.bfloat16
STEP = 512
ROWS = 21
PAIRS = ((0, 0), (0, 1), (0, 2), (1, 1), (1, 2), (2, 2))


def one_hot(ids, count):
    rows = lax.broadcasted_iota(jnp.int32, (count, ids.shape[1]), 0)
    return jnp.where(rows == ids, 1.0, 0.0).astype(BF16)


def pieces(values, count):
    found = []
    for _ in range(count - 1):
        found.append(values.astype(BF16).astype(F32))
        values = values - found[-1]
    return jnp.concatenate(found + [values], 0).astype(BF16)


def unstack(sums, count):
    m = sums.shape[0] // count
    total = sums[0:m]
    for i in range(1, count):
        total = total + sums[i * m : (i + 1) * m]
    return total


def collect(values, chosen_t, count=2):
    return jnp.dot(pieces(values, count), chosen_t, preferred_element_type=F32)


def fetch(stacked, chosen):
    return unstack(jnp.dot(stacked, chosen, preferred_element_type=F32), 2)


def col_sum(values):
    return jnp.sum(values, axis=0, keepdims=True)


def total(values):
    return jnp.sum(values, keepdims=True)


def lane_blocks(row):
    out = row[:, 0:128]
    for b in range(1, row.shape[1] // 128):
        out = out + row[:, b * 128 : (b + 1) * 128]
    return out


def spans(n):
    return [(lo, min(lo + STEP, n)) for lo in range(0, n, STEP)]


def added(sums, more):
    return more if sums is None else sums + more


def scalar_row(values):
    lanes = lax.broadcasted_iota(jnp.int32, (1, 128), 1)
    row = jnp.broadcast_to(values[0], (1, 128))
    for i in range(1, len(values)):
        row = jnp.where(lanes < 32 * i, row, values[i])
    return row


def scalars(row, count):
    return [row[:, 32 * i : 32 * i + 1] for i in range(count)]


def put_rows(ref, rows):
    for r, row in enumerate(rows):
        ref[r : r + 1, :] = row


def solve_points(inverse, sums):
    c = [inverse[8 * i : 8 * i + 8] for i in range(6)]
    g = [sums[8 * i : 8 * i + 8] for i in range(3)]
    return jnp.concatenate(
        [
            c[0] * g[0] + c[1] * g[1] + c[2] * g[2],
            c[1] * g[0] + c[3] * g[1] + c[4] * g[2],
            c[2] * g[0] + c[4] * g[1] + c[5] * g[2],
        ],
        0,
    )


def slots_of(in_ref, out_ref, r, lo, hi):
    inner = in_ref.shape[1]
    if hi <= inner:
        return in_ref[r : r + 1, lo:hi]
    if lo >= inner:
        return out_ref[r : r + 1, lo - inner : hi - inner]
    return jnp.concatenate([in_ref[r : r + 1, lo:inner], out_ref[r : r + 1, : hi - inner]], 1)


def spread_points(placed_ref, first, second, lo, hi):
    return jnp.concatenate(
        [
            placed_ref[8 * r : 8 * r + 8, lo:hi] * first
            + placed_ref[24 + 8 * r : 32 + 8 * r, lo:hi] * second
            for r in range(3)
        ],
        0,
    )


def pull_points(placed_ref, pulled, first, second, lo, hi):
    def image(base):
        out = placed_ref[base : base + 8, lo:hi] * pulled[0:8]
        out = out + placed_ref[base + 8 : base + 16, lo:hi] * pulled[8:16]
        return col_sum(out + placed_ref[base + 16 : base + 24, lo:hi] * pulled[16:24])

    return first - image(0), second - image(24)


def setup_kernel(*refs):
    inputs, mask, outputs, copies, sems = refs[:8], refs[8], refs[9:21], refs[21:29], refs[29]
    copying = [
        pltpu.make_async_copy(source, copy, sems.at[i])
        for i, (source, copy) in enumerate(zip(inputs, copies))
    ]
    for copy in copying:
        copy.start()
    setup(copying, *copies, mask, *outputs)


def setup(
    copying, point_id_ref, count_ref, point_ref, res_ref, damp_ref, cam_ref, cam_id_ref,
    cam_damp_ref, mask_ref,
    same_ref, cross_ref, damp_out_ref, outer_ref, outer_chosen_ref, outer_chosen_t_ref, outer_sum_ref, placed_ref,
    inverse_ref, chosen_ref, chosen_t_ref, partner_ref,
):
    n = cam_ref.shape[1]
    inner = n - 128
    partner = jnp.bitwise_xor(mask_ref[0], lax.axis_index("group"))
    partner_ref[...] = jnp.broadcast_to(partner, (1, 128)).astype(jnp.int32)
    copying[0].wait()
    ids = point_id_ref[...].reshape(1, n)
    low, high = jnp.bitwise_and(ids, 127), jnp.right_shift(ids, 7)
    for lo, hi in spans(n):
        chosen = one_hot(low[:, lo:hi], 128)
        chosen_ref[:, lo:hi] = chosen
        chosen_t_ref[lo:hi, :] = chosen.T
    lanes = lax.broadcasted_iota(jnp.int32, (1, 128), 1)
    copying[1].wait()
    live = jnp.concatenate(
        [jnp.where(lanes < count_ref[0, b], 1.0, 0.0) for b in range(n // 128)], 1
    )
    copying[2].wait()
    copying[3].wait()
    sums = None
    for lo, hi in spans(n):
        digit = lax.broadcasted_iota(jnp.int32, (8, hi - lo), 0)
        digit = jnp.where(digit == high[:, lo:hi], live[:, lo:hi], 0.0)
        for r in range(6):
            placed_ref[8 * r : 8 * r + 8, lo:hi] = digit * point_ref[r : r + 1, lo:hi]
        part = [placed_ref[8 * r : 8 * r + 8, lo:hi] for r in range(6)]
        terms = [part[a] * part[b] + part[3 + a] * part[3 + b] for a, b in PAIRS]
        terms.append(
            spread_points(placed_ref, res_ref[0:1, lo:hi], res_ref[1:2, lo:hi], lo, hi)
        )
        sums = added(sums, collect(jnp.concatenate(terms, 0), chosen_t_ref[lo:hi, :], 3))
    sums = unstack(sums, 3)
    b = [sums[8 * i : 8 * i + 8] for i in range(6)]
    copying[4].wait()
    for axis, entry in ((0, 0), (1, 3), (2, 5)):
        damp = damp_ref[axis : axis + 1, :]
        b[entry] = b[entry] + jnp.concatenate(
            [damp[:, 128 * h : 128 * h + 128] for h in range(8)], 0
        )
    cof = [
        b[3] * b[5] - b[4] * b[4],
        b[2] * b[4] - b[1] * b[5],
        b[1] * b[4] - b[2] * b[3],
        b[0] * b[5] - b[2] * b[2],
        b[1] * b[2] - b[0] * b[4],
        b[0] * b[3] - b[1] * b[1],
    ]
    det = b[0] * cof[0] + b[1] * cof[1] + b[2] * cof[2]
    inverse = jnp.concatenate([c / det for c in cof], 0)
    inverse_ref[...] = inverse
    stacked = pieces(solve_points(inverse, sums[48:72]), 2)
    copying[5].wait()
    copying[6].wait()
    copying[7].wait()
    damp_out_ref[...] = cam_damp_ref[...]
    cam_ids = cam_id_ref[...].reshape(1, n).astype(F32)
    core = jnp.bitwise_and(lax.axis_index("dev"), 1)
    for lo, hi in spans(n):
        pulled = fetch(stacked, chosen_ref[:, lo:hi])
        first, second = pull_points(
            placed_ref, pulled, res_ref[0:1, lo:hi], res_ref[1:2, lo:hi], lo, hi
        )
        rows = cam_ref[:, lo:hi] * live[:, lo:hi]
        every = jnp.concatenate(
            [rows, first, second, cam_ids[:, lo:hi], jnp.zeros((3, hi - lo), F32)], 0
        )
        for at in range(lo, min(hi, inner), 256):
            even = every[:ROWS, at - lo : at - lo + 128]
            odd = every[:ROWS, at - lo + 128 : at - lo + 256]
            i = ROWS * (at // 256)
            same_ref[i : i + ROWS, :] = jnp.where(core == 0, even, odd)
            cross_ref[i : i + ROWS, :] = jnp.where(core == 0, odd, even)
        if hi > inner:
            block = every[:, inner - lo :]
            outer_ref[...] = block
            outer_chosen = ids_of(block)
            outer_chosen_ref[...] = outer_chosen
            outer_chosen_t_ref[...] = outer_chosen.T
            outer_sum_ref[...] = both_halves(start_terms(block, outer_chosen.T))


def ids_of(owned):
    return one_hot(owned[20:21].astype(jnp.int32), 128)


def spread_cams(owned, first, second):
    row = lax.broadcasted_iota(jnp.int32, owned.shape, 0)
    return owned * jnp.where(row < 9, first, jnp.where(row < 18, second, 0.0))


def halves(sums):
    return sums[0:9] + sums[9:18]


def start_terms(owned, chosen_t):
    row = lax.broadcasted_iota(jnp.int32, owned.shape, 0)
    squares = jnp.where(row < 18, owned * owned, 0.0)
    terms = jnp.concatenate([spread_cams(owned, owned[18:19], owned[19:20]), squares], 0)
    return collect(terms, chosen_t)


def both_halves(sums):
    sums = unstack(sums, 2)
    return jnp.concatenate([halves(sums[0:24]), halves(sums[24:48])], 0)


def inner_of(pay_ref):
    return pay_ref.shape[0] // ROWS * 128


def owned_of(pay_ref, lo, hi):
    rows = [pay_ref[ROWS * i : ROWS * i + ROWS, :] for i in range(lo // 128, hi // 128)]
    return jnp.concatenate([jnp.concatenate(rows, 1), jnp.zeros((24 - ROWS, hi - lo), F32)], 0)


def merge_kernel(same_ref, crossed_ref, both_ref):
    for i in range(0, same_ref.shape[0], ROWS):
        both_ref[2 * i : 2 * i + ROWS, :] = same_ref[i : i + ROWS, :]
        both_ref[2 * i + ROWS : 2 * i + 2 * ROWS, :] = crossed_ref[i : i + ROWS, :]


def start_sum_kernel(
    got_ref, outer_sum_ref, damp_ref, group_ref, chosen_ref, chosen_t_ref, pay_ref
):
    core = jnp.bitwise_and(lax.axis_index("dev"), 1)
    sums = None
    for lo, hi in spans(inner_of(pay_ref)):
        for i in range(ROWS * (lo // 128), ROWS * (hi // 128), 2 * ROWS):
            first = got_ref[i : i + ROWS, :]
            second = got_ref[i + ROWS : i + 2 * ROWS, :]
            pay_ref[i : i + ROWS, :] = jnp.where(core == 0, first, second)
            pay_ref[i + ROWS : i + 2 * ROWS, :] = jnp.where(core == 0, second, first)
        owned = owned_of(pay_ref, lo, hi)
        chosen = ids_of(owned)
        chosen_ref[:, lo:hi] = chosen
        chosen_t = chosen.T
        chosen_t_ref[lo:hi, :] = chosen_t
        sums = added(sums, start_terms(owned, chosen_t))
    sums = both_halves(sums)
    for i in range(group_ref.shape[0]):
        group_ref[i, 0:9, :] = sums[0:9]
        group_ref[i, 9:18, :] = sums[9:18] + damp_ref[...]
        group_ref[i, 18:36, :] = outer_sum_ref[...]


def twice(values):
    return pieces(jnp.concatenate([values, values, jnp.zeros((6, 128), F32)], 0), 2)


def apply_cams(owned, stacked, chosen):
    product = owned * fetch(stacked, chosen)
    row = lax.broadcasted_iota(jnp.int32, (8, owned.shape[1]), 0)
    middle = product[8:16]
    first = col_sum(product[0:8] + jnp.where(row == 0, middle, 0.0))
    second = col_sum(product[16:24] + jnp.where(row == 0, 0.0, middle))
    return first, second


def put_moved(in_ref, out_ref, pay_ref, chosen_ref, outer_ref, outer_chosen_ref, own, twin):
    stacked = twice(own)
    for lo, hi in spans(inner_of(pay_ref)):
        moved = apply_cams(owned_of(pay_ref, lo, hi), stacked, chosen_ref[:, lo:hi])
        in_ref[0:1, lo:hi], in_ref[1:2, lo:hi] = moved
    put_rows(out_ref, apply_cams(outer_ref[...], twice(twin), outer_chosen_ref[...]))


def partner_block(partner_ref, group_ref, lo, hi):
    partner = partner_ref[...]
    out = group_ref[0, lo:hi, :]
    for i in range(1, group_ref.shape[0]):
        out = jnp.where(partner == i, group_ref[i, lo:hi, :], out)
    return out


def start_kernel(
    partner_ref, group_ref, sent_ref, outer_sum_ref, pay_ref, chosen_ref, outer_ref,
    outer_chosen_ref,
    in_ref, out_ref, rem_ref, pre_ref, dir_ref,
):
    theirs = partner_block(partner_ref, group_ref, 0, 36)
    sums = [sent_ref[0, 0:18, :] + theirs[18:36], theirs[0:18] + outer_sum_ref[...]]
    for i in range(2):
        remainder = -sums[i][0:9]
        precond = 1.0 / sums[i][9:18]
        rem_ref[i] = remainder
        pre_ref[i] = precond
        dir_ref[i] = precond * remainder
    put_moved(
        in_ref, out_ref, pay_ref, chosen_ref, outer_ref, outer_chosen_ref, dir_ref[0], dir_ref[1]
    )


def point_side(
    in_ref, out_ref, placed_ref, chosen_ref, chosen_t_ref, inverse_ref, outer_ref,
    outer_chosen_t_ref, back_ref, outer_sum_ref, values,
):
    n = placed_ref.shape[1]
    inner = n - 128
    sums = None
    for lo, hi in spans(n):
        first, second = slots_of(in_ref, out_ref, 0, lo, hi), slots_of(in_ref, out_ref, 1, lo, hi)
        terms = spread_points(placed_ref, first, second, lo, hi)
        sums = added(sums, collect(terms, chosen_t_ref[lo:hi, :]))
    stacked = pieces(solve_points(inverse_ref[...], unstack(sums, 2)), 2)
    bend = None
    for lo, hi in spans(n):
        first, second = slots_of(in_ref, out_ref, 0, lo, hi), slots_of(in_ref, out_ref, 1, lo, hi)
        pulled = fetch(stacked, chosen_ref[:, lo:hi])
        kept = pull_points(placed_ref, pulled, first, second, lo, hi)
        bend = added(bend, lane_blocks(first * kept[0] + second * kept[1]))
        for at in range(lo, hi, 128):
            rows = [k[:, at - lo : at - lo + 128] for k in kept]
            if at < inner:
                i = 3 * (at // 128)
                back_ref[i : i + 1, :], back_ref[i + 1 : i + 2, :] = rows
            else:
                spread = spread_cams(outer_ref[...], *rows)
                outer = collect(spread, outer_chosen_t_ref[...])
                outer_sum_ref[...] = halves(unstack(outer, 2))
    values[1] = values[1] + total(bend)
    row = scalar_row(values)
    for i in range(inner // 128):
        back_ref[3 * i + 2 : 3 * i + 3, :] = row


def point_first_kernel(
    in_ref, out_ref, placed_ref, chosen_ref, chosen_t_ref, inverse_ref, outer_ref,
    outer_chosen_t_ref, damp_ref,
    rem_ref, dir_ref,
    back_ref, outer_sum_ref,
):
    direction = dir_ref[0]
    values = [total(rem_ref[0] * direction), total(damp_ref[...] * direction * direction)]
    point_side(
        in_ref, out_ref, placed_ref, chosen_ref, chosen_t_ref, inverse_ref, outer_ref,
        outer_chosen_t_ref, back_ref, outer_sum_ref, values,
    )


def point_next_kernel(
    in_ref, out_ref, placed_ref, chosen_ref, chosen_t_ref, inverse_ref, outer_ref,
    outer_chosen_t_ref, damp_ref,
    rem_ref, scaled_ref, image_ref,
    back_ref, outer_sum_ref,
):
    scaled = scaled_ref[0]
    values = [
        total(rem_ref[0] * scaled),
        total(damp_ref[...] * scaled * scaled),
        total(image_ref[...] * scaled),
    ]
    point_side(
        in_ref, out_ref, placed_ref, chosen_ref, chosen_t_ref, inverse_ref, outer_ref,
        outer_chosen_t_ref, back_ref, outer_sum_ref, values,
    )


def back_row(back_ref, r, lo, hi):
    rows = [back_ref[3 * i + r : 3 * i + r + 1, :] for i in range(lo // 128, hi // 128)]
    return jnp.concatenate(rows, 1)


def inner_image(back_ref, pay_ref, chosen_t_ref, damp_ref, field):
    sums = None
    row = None
    for lo, hi in spans(inner_of(pay_ref)):
        first, second = back_row(back_ref, 0, lo, hi), back_row(back_ref, 1, lo, hi)
        spread = spread_cams(owned_of(pay_ref, lo, hi), first, second)
        sums = added(sums, collect(spread, chosen_t_ref[lo:hi, :]))
        row = added(row, lane_blocks(back_row(back_ref, 2, lo, hi)))
    return damp_ref[...] * field + halves(unstack(sums, 2)), row


def image_kernel(back_ref, outer_sum_ref, pay_ref, chosen_t_ref, damp_ref, dir_ref, group_ref):
    image, partial = inner_image(back_ref, pay_ref, chosen_t_ref, damp_ref, dir_ref[0])
    for i in range(group_ref.shape[0]):
        group_ref[i, 0:9, :] = image
        group_ref[i, 9:18, :] = outer_sum_ref[...]
        group_ref[i, 18:19, :] = partial


def group_total(group_ref, r):
    row = group_ref[0, r : r + 1, :]
    for i in range(1, group_ref.shape[0]):
        row = row + group_ref[i, r : r + 1, :]
    return row


def camera_kernel(
    partner_ref, group_ref, sent_ref, outer_sum_ref, pay_ref, chosen_ref, outer_ref,
    outer_chosen_ref, rem_ref, pre_ref, dir_ref,
    in_ref, out_ref, next_rem_ref, scaled_ref, image_ref, sums_ref,
):
    sums = group_total(group_ref, 18)
    sums_ref[...] = sums
    norm, bend = scalars(sums, 2)
    step = norm / bend
    theirs = partner_block(partner_ref, group_ref, 0, 18)
    images = [sent_ref[0, 0:9, :] + theirs[9:18], theirs[0:9] + outer_sum_ref[...]]
    image_ref[...] = images[0]
    for i in range(2):
        remainder = rem_ref[i] - step * images[i]
        next_rem_ref[i] = remainder
        scaled_ref[i] = pre_ref[i] * remainder
    put_moved(
        in_ref, out_ref, pay_ref, chosen_ref, outer_ref, outer_chosen_ref,
        scaled_ref[0], scaled_ref[1],
    )


def pair_kernel(
    back_ref, outer_sum_ref, pay_ref, chosen_t_ref, damp_ref, scaled_ref, group_ref, image_ref
):
    image, partial = inner_image(back_ref, pay_ref, chosen_t_ref, damp_ref, scaled_ref[0])
    image_ref[...] = image
    for i in range(group_ref.shape[0]):
        group_ref[i, 0:9, :] = outer_sum_ref[...]
        group_ref[i, 9:10, :] = partial


def last_kernel(
    partner_ref, group_ref, inner_ref, rem_ref, scaled_ref, dir_ref, image_ref, sums_ref,
    update_ref, next_rem_ref,
):
    norm, bend = scalars(sums_ref[...], 2)
    next_norm, next_bend, cross = scalars(group_total(group_ref, 9), 3)
    ratio = next_norm / norm
    next_bend = next_bend + ratio * (2.0 * cross + ratio * bend)
    step = next_norm / next_bend
    theirs = partner_block(partner_ref, group_ref, 0, 9)
    image = inner_ref[...] + theirs + ratio * image_ref[...]
    direction = dir_ref[0]
    update_ref[...] = norm / bend * direction + step * (scaled_ref[0] + ratio * direction)
    next_rem_ref[...] = rem_ref[0] - step * image


def call(kernel, name, shapes, *args):
    vmem = pl.BlockSpec(memory_space=pltpu.VMEM)
    return pl.pallas_call(
        kernel,
        name=name,
        out_shape=[jax.ShapeDtypeStruct(*shape) for shape in shapes],
        in_specs=[vmem] * len(args),
        out_specs=[vmem] * len(shapes),
        compiler_params=pltpu.CompilerParams(vmem_limit_bytes=32 * 1024 * 1024),
    )(*args)


def start(*args):
    n = args[0].shape[0]
    shapes = [
        ((ROWS * (n // 256), 128), F32),
        ((ROWS * (n // 256), 128), F32),
        ((9, 128), F32),
        ((24, 128), F32),
        ((128, 128), BF16),
        ((128, 128), BF16),
        ((18, 128), F32),
        ((48, n), F32),
        ((48, 128), F32),
        ((128, n), BF16),
        ((n, 128), BF16),
        ((1, 128), jnp.int32),
    ]
    copies = [
        pltpu.SMEM(a.shape, a.dtype) if i == 1 else pltpu.VMEM(a.shape, a.dtype)
        for i, a in enumerate(args[:-1])
    ]
    args = [pltpu.with_memory_space_constraint(a, pltpu.HBM) for a in args[:-1]] + [args[-1]]
    return pl.pallas_call(
        setup_kernel,
        name="setup",
        out_shape=[jax.ShapeDtypeStruct(*shape) for shape in shapes],
        in_specs=[pl.BlockSpec(memory_space=pltpu.HBM)] * len(copies)
        + [pl.BlockSpec(memory_space=pltpu.SMEM)],
        out_specs=[pl.BlockSpec(memory_space=pltpu.VMEM)] * len(shapes),
        scratch_shapes=copies + [pltpu.SemaphoreType.DMA((len(copies),))],
        compiler_params=pltpu.CompilerParams(vmem_limit_bytes=32 * 1024 * 1024),
    )(*args)


def on_device(
    cam_jac, point_jac, residuals, obs_camera, obs_point, obs_count, cam_damp, pt_damp, partner_mask
):
    n = cam_jac.shape[1]
    inner = n - 128
    groups = lax.axis_size("group")

    def over_dev(values):
        return lax.all_to_all(values, "dev", split_axis=1, concat_axis=1, tiled=True)

    def rows_over_dev(values):
        blocks = values.reshape(inner // 128, -1, 1, 128)
        got = lax.all_to_all(blocks, "dev", split_axis=0, concat_axis=0, tiled=True)
        return got.reshape(values.shape)

    def over_chips(same, cross):
        count = lax.axis_size("dev")
        crossed = lax.ppermute(cross, "dev", [(i, i ^ 1) for i in range(count)])
        (both,) = call(merge_kernel, "merge", [((ROWS * count, 128), F32)], same, crossed)
        got = lax.all_to_all(
            both.reshape(count // 2, 2 * ROWS, 1, 128), "dev", split_axis=0, concat_axis=0, tiled=True,
            axis_index_groups=[list(range(c, count, 2)) for c in range(2)],
        )
        return got.reshape(-1, 128)

    def over_group(values):
        return lax.all_to_all(values, "group", split_axis=0, concat_axis=0, tiled=True)

    def sends(rows):
        return ((groups, rows, 128), F32)

    field, fields, line = ((9, 128), F32), ((2, 9, 128), F32), ((1, 128), F32)
    pair, back = [((2, inner), F32), ((2, 128), F32)], ((inner // 128 * 3, 128), F32)
    (
        same, cross, cam_damp, outer, outer_chosen, outer_chosen_t, outer_sum, placed, inverse,
        *ones, partner,
    ) = start(
        obs_point, obs_count, point_jac, residuals, pt_damp, cam_jac, obs_camera, cam_damp,
        partner_mask,
    )
    pay = over_chips(same, cross)
    sums, chosen, chosen_t, pay = call(
        start_sum_kernel, "start_sum",
        [sends(36), ((128, inner), BF16), ((inner, 128), BF16), (pay.shape, F32)],
        pay, outer_sum, cam_damp,
    )
    cameras = (pay, chosen, outer, outer_chosen)
    moved, outer_moved, remainder, precond, direction = call(
        start_kernel, "start", pair + [fields] * 3,
        partner, over_group(sums), sums, outer_sum, *cameras,
    )
    points = (placed, *ones, inverse, outer, outer_chosen_t, cam_damp)
    kept, outer_sum = call(
        point_first_kernel, "point_first", [back, field],
        over_dev(moved), outer_moved, *points, remainder, direction,
    )
    kept = rows_over_dev(kept)
    (images,) = call(
        image_kernel, "image", [sends(19)], kept, outer_sum, pay, chosen_t, cam_damp, direction
    )
    moved, outer_moved, remainder, scaled, image, totals = call(
        camera_kernel, "camera", pair + [fields] * 2 + [field, line],
        partner, over_group(images), images, outer_sum, *cameras, remainder, precond, direction,
    )
    kept, outer_sum = call(
        point_next_kernel, "point_next", [back, field],
        over_dev(moved), outer_moved, *points, remainder, scaled, image,
    )
    kept = rows_over_dev(kept)
    images, next_image = call(
        pair_kernel, "pair", [sends(10), field], kept, outer_sum, pay, chosen_t, cam_damp, scaled
    )
    update, remainder = call(
        last_kernel, "last", [field] * 2,
        partner, over_group(images), next_image, remainder, scaled, direction, image, totals,
    )
    return (update, remainder)


def solution(mesh):
    slots, rows = P(None, ("group", "dev")), P(("group", "dev"))
    return jax.shard_map(
        on_device,
        mesh=mesh,
        in_specs=(
            slots, slots, slots, rows, rows, P(("group", "dev"), None), slots, slots, P("dev"),
        ),
        out_specs=(slots, slots),
        check_vma=False,
    )
```

```python
import jax
import jax.numpy as jnp
from jax import lax
from jax.experimental import pallas as pl
from jax.experimental.pallas import tpu as pltpu
from jax.sharding import PartitionSpec as P

F32 = jnp.float32
BF16 = jnp.bfloat16
STEP = 512
ROWS = 21
PAIRS = ((0, 0), (0, 1), (0, 2), (1, 1), (1, 2), (2, 2))


def one_hot(ids, count):
    rows = lax.broadcasted_iota(jnp.int32, (count, ids.shape[1]), 0)
    return jnp.where(rows == ids, 1.0, 0.0).astype(BF16)


def pieces(values, count):
    found = []
    for _ in range(count - 1):
        found.append(values.astype(BF16).astype(F32))
        values = values - found[-1]
    return jnp.concatenate(found + [values], 0).astype(BF16)


def unstack(sums, count):
    m = sums.shape[0] // count
    total = sums[0:m]
    for i in range(1, count):
        total = total + sums[i * m : (i + 1) * m]
    return total


def collect(values, chosen_t, count=2):
    return jnp.dot(pieces(values, count), chosen_t, preferred_element_type=F32)


def fetch(stacked, chosen):
    return unstack(jnp.dot(stacked, chosen, preferred_element_type=F32), 2)


def col_sum(values):
    return jnp.sum(values, axis=0, keepdims=True)


def total(values):
    return jnp.sum(values, keepdims=True)


def lane_blocks(row):
    out = row[:, 0:128]
    for b in range(1, row.shape[1] // 128):
        out = out + row[:, b * 128 : (b + 1) * 128]
    return out


def spans(n):
    return [(lo, min(lo + STEP, n)) for lo in range(0, n, STEP)]


def added(sums, more):
    return more if sums is None else sums + more


def scalar_row(values):
    lanes = lax.broadcasted_iota(jnp.int32, (1, 128), 1)
    row = jnp.broadcast_to(values[0], (1, 128))
    for i in range(1, len(values)):
        row = jnp.where(lanes < 32 * i, row, values[i])
    return row


def scalars(row, count):
    return [row[:, 32 * i : 32 * i + 1] for i in range(count)]


def put_rows(ref, rows):
    for r, row in enumerate(rows):
        ref[r : r + 1, :] = row


def solve_points(inverse, sums):
    c = [inverse[8 * i : 8 * i + 8] for i in range(6)]
    g = [sums[8 * i : 8 * i + 8] for i in range(3)]
    return jnp.concatenate(
        [
            c[0] * g[0] + c[1] * g[1] + c[2] * g[2],
            c[1] * g[0] + c[3] * g[1] + c[4] * g[2],
            c[2] * g[0] + c[4] * g[1] + c[5] * g[2],
        ],
        0,
    )


def slots_of(in_ref, out_ref, r, lo, hi):
    inner = in_ref.shape[1]
    if hi <= inner:
        return in_ref[r : r + 1, lo:hi]
    if lo >= inner:
        return out_ref[r : r + 1, lo - inner : hi - inner]
    return jnp.concatenate([in_ref[r : r + 1, lo:inner], out_ref[r : r + 1, : hi - inner]], 1)


def spread_points(placed_ref, first, second, lo, hi):
    return jnp.concatenate(
        [
            placed_ref[8 * r : 8 * r + 8, lo:hi] * first
            + placed_ref[24 + 8 * r : 32 + 8 * r, lo:hi] * second
            for r in range(3)
        ],
        0,
    )


def pull_points(placed_ref, pulled, first, second, lo, hi):
    def image(base):
        out = placed_ref[base : base + 8, lo:hi] * pulled[0:8]
        out = out + placed_ref[base + 8 : base + 16, lo:hi] * pulled[8:16]
        return col_sum(out + placed_ref[base + 16 : base + 24, lo:hi] * pulled[16:24])

    return first - image(0), second - image(24)


def setup_kernel(*refs):
    inputs, mask, outputs, copies, sems = refs[:8], refs[8], refs[9:20], refs[20:28], refs[28]
    copying = [
        pltpu.make_async_copy(source, copy, sems.at[i])
        for i, (source, copy) in enumerate(zip(inputs, copies))
    ]
    for copy in copying:
        copy.start()
    setup(copying, *copies, mask, *outputs)


def setup(
    copying, point_id_ref, count_ref, point_ref, res_ref, damp_ref, cam_ref, cam_id_ref,
    cam_damp_ref, mask_ref,
    in_ref, damp_out_ref, outer_ref, outer_chosen_ref, outer_chosen_t_ref, outer_sum_ref, placed_ref,
    inverse_ref, chosen_ref, chosen_t_ref, partner_ref,
):
    n = cam_ref.shape[1]
    inner = n - 128
    partner = jnp.bitwise_xor(mask_ref[0], lax.axis_index("group"))
    partner_ref[...] = jnp.broadcast_to(partner, (1, 128)).astype(jnp.int32)
    copying[0].wait()
    ids = point_id_ref[...].reshape(1, n)
    low, high = jnp.bitwise_and(ids, 127), jnp.right_shift(ids, 7)
    for lo, hi in spans(n):
        chosen = one_hot(low[:, lo:hi], 128)
        chosen_ref[:, lo:hi] = chosen
        chosen_t_ref[lo:hi, :] = chosen.T
    lanes = lax.broadcasted_iota(jnp.int32, (1, 128), 1)
    copying[1].wait()
    live = jnp.concatenate(
        [jnp.where(lanes < count_ref[0, b], 1.0, 0.0) for b in range(n // 128)], 1
    )
    copying[2].wait()
    copying[3].wait()
    sums = None
    for lo, hi in spans(n):
        digit = lax.broadcasted_iota(jnp.int32, (8, hi - lo), 0)
        digit = jnp.where(digit == high[:, lo:hi], live[:, lo:hi], 0.0)
        for r in range(6):
            placed_ref[8 * r : 8 * r + 8, lo:hi] = digit * point_ref[r : r + 1, lo:hi]
        part = [placed_ref[8 * r : 8 * r + 8, lo:hi] for r in range(6)]
        terms = [part[a] * part[b] + part[3 + a] * part[3 + b] for a, b in PAIRS]
        terms.append(
            spread_points(placed_ref, res_ref[0:1, lo:hi], res_ref[1:2, lo:hi], lo, hi)
        )
        sums = added(sums, collect(jnp.concatenate(terms, 0), chosen_t_ref[lo:hi, :], 3))
    sums = unstack(sums, 3)
    b = [sums[8 * i : 8 * i + 8] for i in range(6)]
    copying[4].wait()
    for axis, entry in ((0, 0), (1, 3), (2, 5)):
        damp = damp_ref[axis : axis + 1, :]
        b[entry] = b[entry] + jnp.concatenate(
            [damp[:, 128 * h : 128 * h + 128] for h in range(8)], 0
        )
    cof = [
        b[3] * b[5] - b[4] * b[4],
        b[2] * b[4] - b[1] * b[5],
        b[1] * b[4] - b[2] * b[3],
        b[0] * b[5] - b[2] * b[2],
        b[1] * b[2] - b[0] * b[4],
        b[0] * b[3] - b[1] * b[1],
    ]
    det = b[0] * cof[0] + b[1] * cof[1] + b[2] * cof[2]
    inverse = jnp.concatenate([c / det for c in cof], 0)
    inverse_ref[...] = inverse
    stacked = pieces(solve_points(inverse, sums[48:72]), 2)
    copying[5].wait()
    copying[6].wait()
    copying[7].wait()
    damp_out_ref[...] = cam_damp_ref[...]
    cam_ids = cam_id_ref[...].reshape(1, n).astype(F32)
    for lo, hi in spans(n):
        pulled = fetch(stacked, chosen_ref[:, lo:hi])
        first, second = pull_points(
            placed_ref, pulled, res_ref[0:1, lo:hi], res_ref[1:2, lo:hi], lo, hi
        )
        rows = cam_ref[:, lo:hi] * live[:, lo:hi]
        every = jnp.concatenate(
            [rows, first, second, cam_ids[:, lo:hi], jnp.zeros((3, hi - lo), F32)], 0
        )
        for at in range(lo, hi, 128):
            block = every[:, at - lo : at - lo + 128]
            if at < inner:
                i = at // 128
                in_ref[ROWS * i : ROWS * i + ROWS, :] = block[:ROWS]
            else:
                outer_ref[...] = block
                outer_chosen = ids_of(block)
                outer_chosen_ref[...] = outer_chosen
                outer_chosen_t_ref[...] = outer_chosen.T
                outer_sum_ref[...] = both_halves(start_terms(block, outer_chosen.T))


def ids_of(owned):
    return one_hot(owned[20:21].astype(jnp.int32), 128)


def spread_cams(owned, first, second):
    row = lax.broadcasted_iota(jnp.int32, owned.shape, 0)
    return owned * jnp.where(row < 9, first, jnp.where(row < 18, second, 0.0))


def halves(sums):
    return sums[0:9] + sums[9:18]


def start_terms(owned, chosen_t):
    row = lax.broadcasted_iota(jnp.int32, owned.shape, 0)
    squares = jnp.where(row < 18, owned * owned, 0.0)
    terms = jnp.concatenate([spread_cams(owned, owned[18:19], owned[19:20]), squares], 0)
    return collect(terms, chosen_t)


def both_halves(sums):
    sums = unstack(sums, 2)
    return jnp.concatenate([halves(sums[0:24]), halves(sums[24:48])], 0)


def inner_of(pay_ref):
    return pay_ref.shape[0] // ROWS * 128


def owned_of(pay_ref, lo, hi):
    rows = [pay_ref[ROWS * i : ROWS * i + ROWS, :] for i in range(lo // 128, hi // 128)]
    return jnp.concatenate([jnp.concatenate(rows, 1), jnp.zeros((24 - ROWS, hi - lo), F32)], 0)


def start_sum_kernel(pay_ref, outer_sum_ref, damp_ref, group_ref, chosen_ref, chosen_t_ref):
    sums = None
    for lo, hi in spans(inner_of(pay_ref)):
        owned = owned_of(pay_ref, lo, hi)
        chosen = ids_of(owned)
        chosen_ref[:, lo:hi] = chosen
        chosen_t = chosen.T
        chosen_t_ref[lo:hi, :] = chosen_t
        sums = added(sums, start_terms(owned, chosen_t))
    sums = both_halves(sums)
    for i in range(group_ref.shape[0]):
        group_ref[i, 0:9, :] = sums[0:9]
        group_ref[i, 9:18, :] = sums[9:18] + damp_ref[...]
        group_ref[i, 18:36, :] = outer_sum_ref[...]


def twice(values):
    return pieces(jnp.concatenate([values, values, jnp.zeros((6, 128), F32)], 0), 2)


def apply_cams(owned, stacked, chosen):
    product = owned * fetch(stacked, chosen)
    row = lax.broadcasted_iota(jnp.int32, (8, owned.shape[1]), 0)
    middle = product[8:16]
    first = col_sum(product[0:8] + jnp.where(row == 0, middle, 0.0))
    second = col_sum(product[16:24] + jnp.where(row == 0, 0.0, middle))
    return first, second


def put_moved(in_ref, out_ref, pay_ref, chosen_ref, outer_ref, outer_chosen_ref, own, twin):
    stacked = twice(own)
    for lo, hi in spans(inner_of(pay_ref)):
        moved = apply_cams(owned_of(pay_ref, lo, hi), stacked, chosen_ref[:, lo:hi])
        in_ref[0:1, lo:hi], in_ref[1:2, lo:hi] = moved
    put_rows(out_ref, apply_cams(outer_ref[...], twice(twin), outer_chosen_ref[...]))


def partner_block(partner_ref, group_ref, lo, hi):
    partner = partner_ref[...]
    out = group_ref[0, lo:hi, :]
    for i in range(1, group_ref.shape[0]):
        out = jnp.where(partner == i, group_ref[i, lo:hi, :], out)
    return out


def start_kernel(
    partner_ref, group_ref, sent_ref, outer_sum_ref, pay_ref, chosen_ref, outer_ref,
    outer_chosen_ref,
    in_ref, out_ref, rem_ref, pre_ref, dir_ref,
):
    theirs = partner_block(partner_ref, group_ref, 0, 36)
    sums = [sent_ref[0, 0:18, :] + theirs[18:36], theirs[0:18] + outer_sum_ref[...]]
    for i in range(2):
        remainder = -sums[i][0:9]
        precond = 1.0 / sums[i][9:18]
        rem_ref[i] = remainder
        pre_ref[i] = precond
        dir_ref[i] = precond * remainder
    put_moved(
        in_ref, out_ref, pay_ref, chosen_ref, outer_ref, outer_chosen_ref, dir_ref[0], dir_ref[1]
    )


def point_side(
    in_ref, out_ref, placed_ref, chosen_ref, chosen_t_ref, inverse_ref, outer_ref,
    outer_chosen_t_ref, back_ref, outer_sum_ref, values,
):
    n = placed_ref.shape[1]
    inner = n - 128
    sums = None
    for lo, hi in spans(n):
        first, second = slots_of(in_ref, out_ref, 0, lo, hi), slots_of(in_ref, out_ref, 1, lo, hi)
        terms = spread_points(placed_ref, first, second, lo, hi)
        sums = added(sums, collect(terms, chosen_t_ref[lo:hi, :]))
    stacked = pieces(solve_points(inverse_ref[...], unstack(sums, 2)), 2)
    bend = None
    for lo, hi in spans(n):
        first, second = slots_of(in_ref, out_ref, 0, lo, hi), slots_of(in_ref, out_ref, 1, lo, hi)
        pulled = fetch(stacked, chosen_ref[:, lo:hi])
        kept = pull_points(placed_ref, pulled, first, second, lo, hi)
        bend = added(bend, lane_blocks(first * kept[0] + second * kept[1]))
        for at in range(lo, hi, 128):
            rows = [k[:, at - lo : at - lo + 128] for k in kept]
            if at < inner:
                i = 3 * (at // 128)
                back_ref[i : i + 1, :], back_ref[i + 1 : i + 2, :] = rows
            else:
                spread = spread_cams(outer_ref[...], *rows)
                outer = collect(spread, outer_chosen_t_ref[...])
                outer_sum_ref[...] = halves(unstack(outer, 2))
    values[1] = values[1] + total(bend)
    row = scalar_row(values)
    for i in range(inner // 128):
        back_ref[3 * i + 2 : 3 * i + 3, :] = row


def point_first_kernel(
    in_ref, out_ref, placed_ref, chosen_ref, chosen_t_ref, inverse_ref, outer_ref,
    outer_chosen_t_ref, damp_ref,
    rem_ref, dir_ref,
    back_ref, outer_sum_ref,
):
    direction = dir_ref[0]
    values = [total(rem_ref[0] * direction), total(damp_ref[...] * direction * direction)]
    point_side(
        in_ref, out_ref, placed_ref, chosen_ref, chosen_t_ref, inverse_ref, outer_ref,
        outer_chosen_t_ref, back_ref, outer_sum_ref, values,
    )


def point_next_kernel(
    in_ref, out_ref, placed_ref, chosen_ref, chosen_t_ref, inverse_ref, outer_ref,
    outer_chosen_t_ref, damp_ref,
    rem_ref, scaled_ref, image_ref,
    back_ref, outer_sum_ref,
):
    scaled = scaled_ref[0]
    values = [
        total(rem_ref[0] * scaled),
        total(damp_ref[...] * scaled * scaled),
        total(image_ref[...] * scaled),
    ]
    point_side(
        in_ref, out_ref, placed_ref, chosen_ref, chosen_t_ref, inverse_ref, outer_ref,
        outer_chosen_t_ref, back_ref, outer_sum_ref, values,
    )


def back_row(back_ref, r, lo, hi):
    rows = [back_ref[3 * i + r : 3 * i + r + 1, :] for i in range(lo // 128, hi // 128)]
    return jnp.concatenate(rows, 1)


def inner_image(back_ref, pay_ref, chosen_t_ref, damp_ref, field):
    sums = None
    row = None
    for lo, hi in spans(inner_of(pay_ref)):
        first, second = back_row(back_ref, 0, lo, hi), back_row(back_ref, 1, lo, hi)
        spread = spread_cams(owned_of(pay_ref, lo, hi), first, second)
        sums = added(sums, collect(spread, chosen_t_ref[lo:hi, :]))
        row = added(row, lane_blocks(back_row(back_ref, 2, lo, hi)))
    return damp_ref[...] * field + halves(unstack(sums, 2)), row


def image_kernel(back_ref, outer_sum_ref, pay_ref, chosen_t_ref, damp_ref, dir_ref, group_ref):
    image, partial = inner_image(back_ref, pay_ref, chosen_t_ref, damp_ref, dir_ref[0])
    for i in range(group_ref.shape[0]):
        group_ref[i, 0:9, :] = image
        group_ref[i, 9:18, :] = outer_sum_ref[...]
        group_ref[i, 18:19, :] = partial


def group_total(group_ref, r):
    row = group_ref[0, r : r + 1, :]
    for i in range(1, group_ref.shape[0]):
        row = row + group_ref[i, r : r + 1, :]
    return row


def camera_kernel(
    partner_ref, group_ref, sent_ref, outer_sum_ref, pay_ref, chosen_ref, outer_ref,
    outer_chosen_ref, rem_ref, pre_ref, dir_ref,
    in_ref, out_ref, next_rem_ref, scaled_ref, image_ref, sums_ref,
):
    sums = group_total(group_ref, 18)
    sums_ref[...] = sums
    norm, bend = scalars(sums, 2)
    step = norm / bend
    theirs = partner_block(partner_ref, group_ref, 0, 18)
    images = [sent_ref[0, 0:9, :] + theirs[9:18], theirs[0:9] + outer_sum_ref[...]]
    image_ref[...] = images[0]
    for i in range(2):
        remainder = rem_ref[i] - step * images[i]
        next_rem_ref[i] = remainder
        scaled_ref[i] = pre_ref[i] * remainder
    put_moved(
        in_ref, out_ref, pay_ref, chosen_ref, outer_ref, outer_chosen_ref,
        scaled_ref[0], scaled_ref[1],
    )


def pair_kernel(
    back_ref, outer_sum_ref, pay_ref, chosen_t_ref, damp_ref, scaled_ref, group_ref, image_ref
):
    image, partial = inner_image(back_ref, pay_ref, chosen_t_ref, damp_ref, scaled_ref[0])
    image_ref[...] = image
    for i in range(group_ref.shape[0]):
        group_ref[i, 0:9, :] = outer_sum_ref[...]
        group_ref[i, 9:10, :] = partial


def last_kernel(
    partner_ref, group_ref, inner_ref, rem_ref, scaled_ref, dir_ref, image_ref, sums_ref,
    update_ref, next_rem_ref,
):
    norm, bend = scalars(sums_ref[...], 2)
    next_norm, next_bend, cross = scalars(group_total(group_ref, 9), 3)
    ratio = next_norm / norm
    next_bend = next_bend + ratio * (2.0 * cross + ratio * bend)
    step = next_norm / next_bend
    theirs = partner_block(partner_ref, group_ref, 0, 9)
    image = inner_ref[...] + theirs + ratio * image_ref[...]
    direction = dir_ref[0]
    update_ref[...] = norm / bend * direction + step * (scaled_ref[0] + ratio * direction)
    next_rem_ref[...] = rem_ref[0] - step * image


def call(kernel, name, shapes, *args):
    vmem = pl.BlockSpec(memory_space=pltpu.VMEM)
    return pl.pallas_call(
        kernel,
        name=name,
        out_shape=[jax.ShapeDtypeStruct(*shape) for shape in shapes],
        in_specs=[vmem] * len(args),
        out_specs=[vmem] * len(shapes),
        compiler_params=pltpu.CompilerParams(vmem_limit_bytes=32 * 1024 * 1024),
    )(*args)


def start(*args):
    n = args[0].shape[0]
    shapes = [
        ((ROWS * (n // 128 - 1), 128), F32),
        ((9, 128), F32),
        ((24, 128), F32),
        ((128, 128), BF16),
        ((128, 128), BF16),
        ((18, 128), F32),
        ((48, n), F32),
        ((48, 128), F32),
        ((128, n), BF16),
        ((n, 128), BF16),
        ((1, 128), jnp.int32),
    ]
    copies = [
        pltpu.SMEM(a.shape, a.dtype) if i == 1 else pltpu.VMEM(a.shape, a.dtype)
        for i, a in enumerate(args[:-1])
    ]
    args = [pltpu.with_memory_space_constraint(a, pltpu.HBM) for a in args[:-1]] + [args[-1]]
    return pl.pallas_call(
        setup_kernel,
        name="setup",
        out_shape=[jax.ShapeDtypeStruct(*shape) for shape in shapes],
        in_specs=[pl.BlockSpec(memory_space=pltpu.HBM)] * len(copies)
        + [pl.BlockSpec(memory_space=pltpu.SMEM)],
        out_specs=[pl.BlockSpec(memory_space=pltpu.VMEM)] * len(shapes),
        scratch_shapes=copies + [pltpu.SemaphoreType.DMA((len(copies),))],
        compiler_params=pltpu.CompilerParams(vmem_limit_bytes=32 * 1024 * 1024),
    )(*args)


def on_device(
    cam_jac, point_jac, residuals, obs_camera, obs_point, obs_count, cam_damp, pt_damp, partner_mask
):
    n = cam_jac.shape[1]
    inner = n - 128
    groups = lax.axis_size("group")

    def over_dev(values):
        return lax.all_to_all(values, "dev", split_axis=1, concat_axis=1, tiled=True)

    def rows_over_dev(values):
        blocks = values.reshape(inner // 128, -1, 1, 128)
        got = lax.all_to_all(blocks, "dev", split_axis=0, concat_axis=0, tiled=True)
        return got.reshape(values.shape)

    def over_group(values):
        return lax.all_to_all(values, "group", split_axis=0, concat_axis=0, tiled=True)

    def sends(rows):
        return ((groups, rows, 128), F32)

    field, fields, line = ((9, 128), F32), ((2, 9, 128), F32), ((1, 128), F32)
    pair, back = [((2, inner), F32), ((2, 128), F32)], ((inner // 128 * 3, 128), F32)
    (
        pay, cam_damp, outer, outer_chosen, outer_chosen_t, outer_sum, placed, inverse,
        *ones, partner,
    ) = start(
        obs_point, obs_count, point_jac, residuals, pt_damp, cam_jac, obs_camera, cam_damp,
        partner_mask,
    )
    pay = rows_over_dev(pay)
    sums, chosen, chosen_t = call(
        start_sum_kernel, "start_sum", [sends(36), ((128, inner), BF16), ((inner, 128), BF16)],
        pay, outer_sum, cam_damp,
    )
    cameras = (pay, chosen, outer, outer_chosen)
    moved, outer_moved, remainder, precond, direction = call(
        start_kernel, "start", pair + [fields] * 3,
        partner, over_group(sums), sums, outer_sum, *cameras,
    )
    points = (placed, *ones, inverse, outer, outer_chosen_t, cam_damp)
    kept, outer_sum = call(
        point_first_kernel, "point_first", [back, field],
        over_dev(moved), outer_moved, *points, remainder, direction,
    )
    kept = rows_over_dev(kept)
    (images,) = call(
        image_kernel, "image", [sends(19)], kept, outer_sum, pay, chosen_t, cam_damp, direction
    )
    moved, outer_moved, remainder, scaled, image, totals = call(
        camera_kernel, "camera", pair + [fields] * 2 + [field, line],
        partner, over_group(images), images, outer_sum, *cameras, remainder, precond, direction,
    )
    kept, outer_sum = call(
        point_next_kernel, "point_next", [back, field],
        over_dev(moved), outer_moved, *points, remainder, scaled, image,
    )
    kept = rows_over_dev(kept)
    images, next_image = call(
        pair_kernel, "pair", [sends(10), field], kept, outer_sum, pay, chosen_t, cam_damp, scaled
    )
    update, remainder = call(
        last_kernel, "last", [field] * 2,
        partner, over_group(images), next_image, remainder, scaled, direction, image, totals,
    )
    return (update, remainder)


def solution(mesh):
    slots, rows = P(None, ("group", "dev")), P(("group", "dev"))
    return jax.shard_map(
        on_device,
        mesh=mesh,
        in_specs=(
            slots, slots, slots, rows, rows, P(("group", "dev"), None), slots, slots, P("dev"),
        ),
        out_specs=(slots, slots),
        check_vma=False,
    )
```

```python
import jax
import jax.numpy as jnp
from jax import lax
from jax.experimental import pallas as pl
from jax.experimental.pallas import tpu as pltpu
from jax.sharding import PartitionSpec as P

F32 = jnp.float32
BF16 = jnp.bfloat16
STEP = 512
ROWS = 21
PAIRS = ((0, 0), (0, 1), (0, 2), (1, 1), (1, 2), (2, 2))


def one_hot(ids, count):
    rows = lax.broadcasted_iota(jnp.int32, (count, ids.shape[1]), 0)
    return jnp.where(rows == ids, 1.0, 0.0).astype(BF16)


def pieces(values, count):
    found = []
    for _ in range(count - 1):
        found.append(values.astype(BF16).astype(F32))
        values = values - found[-1]
    return jnp.concatenate(found + [values], 0).astype(BF16)


def unstack(sums, count):
    m = sums.shape[0] // count
    total = sums[0:m]
    for i in range(1, count):
        total = total + sums[i * m : (i + 1) * m]
    return total


def collect(values, chosen_t, count=2):
    return jnp.dot(pieces(values, count), chosen_t, preferred_element_type=F32)


def fetch(stacked, chosen):
    return unstack(jnp.dot(stacked, chosen, preferred_element_type=F32), 2)


def col_sum(values):
    return jnp.sum(values, axis=0, keepdims=True)


def total(values):
    return jnp.sum(values, keepdims=True)


def lane_blocks(row):
    out = row[:, 0:128]
    for b in range(1, row.shape[1] // 128):
        out = out + row[:, b * 128 : (b + 1) * 128]
    return out


def spans(n):
    return [(lo, min(lo + STEP, n)) for lo in range(0, n, STEP)]


def added(sums, more):
    return more if sums is None else sums + more


def scalar_row(values):
    lanes = lax.broadcasted_iota(jnp.int32, (1, 128), 1)
    row = jnp.broadcast_to(values[0], (1, 128))
    for i in range(1, len(values)):
        row = jnp.where(lanes < 32 * i, row, values[i])
    return row


def scalars(row, count):
    return [row[:, 32 * i : 32 * i + 1] for i in range(count)]


def put_rows(ref, rows):
    for r, row in enumerate(rows):
        ref[r : r + 1, :] = row


def solve_points(inverse, sums):
    c = [inverse[8 * i : 8 * i + 8] for i in range(6)]
    g = [sums[8 * i : 8 * i + 8] for i in range(3)]
    return jnp.concatenate(
        [
            c[0] * g[0] + c[1] * g[1] + c[2] * g[2],
            c[1] * g[0] + c[3] * g[1] + c[4] * g[2],
            c[2] * g[0] + c[4] * g[1] + c[5] * g[2],
        ],
        0,
    )


def slots_of(in_ref, out_ref, r, lo, hi):
    inner = in_ref.shape[1]
    if hi <= inner:
        return in_ref[r : r + 1, lo:hi]
    if lo >= inner:
        return out_ref[r : r + 1, lo - inner : hi - inner]
    return jnp.concatenate([in_ref[r : r + 1, lo:inner], out_ref[r : r + 1, : hi - inner]], 1)


def spread_points(placed_ref, first, second, lo, hi):
    return jnp.concatenate(
        [
            placed_ref[8 * r : 8 * r + 8, lo:hi] * first
            + placed_ref[24 + 8 * r : 32 + 8 * r, lo:hi] * second
            for r in range(3)
        ],
        0,
    )


def pull_points(placed_ref, pulled, first, second, lo, hi):
    def image(base):
        out = placed_ref[base : base + 8, lo:hi] * pulled[0:8]
        out = out + placed_ref[base + 8 : base + 16, lo:hi] * pulled[8:16]
        return col_sum(out + placed_ref[base + 16 : base + 24, lo:hi] * pulled[16:24])

    return first - image(0), second - image(24)


def setup_kernel(*refs):
    inputs, mask, outputs, copies, sems = refs[:8], refs[8], refs[9:20], refs[20:28], refs[28]
    copying = [
        pltpu.make_async_copy(source, copy, sems.at[i])
        for i, (source, copy) in enumerate(zip(inputs, copies))
    ]
    for copy in copying:
        copy.start()
    setup(copying, *copies, mask, *outputs)


def setup(
    copying, point_id_ref, count_ref, point_ref, res_ref, damp_ref, cam_ref, cam_id_ref,
    cam_damp_ref, mask_ref,
    in_ref, damp_out_ref, outer_ref, outer_chosen_ref, outer_chosen_t_ref, outer_sum_ref, placed_ref,
    inverse_ref, chosen_ref, chosen_t_ref, partner_ref,
):
    n = cam_ref.shape[1]
    inner = n - 128
    partner = jnp.bitwise_xor(mask_ref[0], lax.axis_index("group"))
    partner_ref[...] = jnp.broadcast_to(partner, (1, 128)).astype(jnp.int32)
    copying[0].wait()
    ids = point_id_ref[...].reshape(1, n)
    low, high = jnp.bitwise_and(ids, 127), jnp.right_shift(ids, 7)
    for lo, hi in spans(n):
        chosen = one_hot(low[:, lo:hi], 128)
        chosen_ref[:, lo:hi] = chosen
        chosen_t_ref[lo:hi, :] = chosen.T
    lanes = lax.broadcasted_iota(jnp.int32, (1, 128), 1)
    copying[1].wait()
    live = jnp.concatenate(
        [jnp.where(lanes < count_ref[0, b], 1.0, 0.0) for b in range(n // 128)], 1
    )
    copying[2].wait()
    copying[3].wait()
    sums = None
    for lo, hi in spans(n):
        digit = lax.broadcasted_iota(jnp.int32, (8, hi - lo), 0)
        digit = jnp.where(digit == high[:, lo:hi], live[:, lo:hi], 0.0)
        for r in range(6):
            placed_ref[8 * r : 8 * r + 8, lo:hi] = digit * point_ref[r : r + 1, lo:hi]
        part = [placed_ref[8 * r : 8 * r + 8, lo:hi] for r in range(6)]
        terms = [part[a] * part[b] + part[3 + a] * part[3 + b] for a, b in PAIRS]
        terms.append(
            spread_points(placed_ref, res_ref[0:1, lo:hi], res_ref[1:2, lo:hi], lo, hi)
        )
        sums = added(sums, collect(jnp.concatenate(terms, 0), chosen_t_ref[lo:hi, :], 3))
    sums = unstack(sums, 3)
    b = [sums[8 * i : 8 * i + 8] for i in range(6)]
    copying[4].wait()
    for axis, entry in ((0, 0), (1, 3), (2, 5)):
        damp = damp_ref[axis : axis + 1, :]
        b[entry] = b[entry] + jnp.concatenate(
            [damp[:, 128 * h : 128 * h + 128] for h in range(8)], 0
        )
    cof = [
        b[3] * b[5] - b[4] * b[4],
        b[2] * b[4] - b[1] * b[5],
        b[1] * b[4] - b[2] * b[3],
        b[0] * b[5] - b[2] * b[2],
        b[1] * b[2] - b[0] * b[4],
        b[0] * b[3] - b[1] * b[1],
    ]
    det = b[0] * cof[0] + b[1] * cof[1] + b[2] * cof[2]
    inverse = jnp.concatenate([c / det for c in cof], 0)
    inverse_ref[...] = inverse
    stacked = pieces(solve_points(inverse, sums[48:72]), 2)
    copying[5].wait()
    copying[6].wait()
    copying[7].wait()
    damp_out_ref[...] = cam_damp_ref[...]
    cam_ids = cam_id_ref[...].reshape(1, n).astype(F32)
    for lo, hi in spans(n):
        pulled = fetch(stacked, chosen_ref[:, lo:hi])
        first, second = pull_points(
            placed_ref, pulled, res_ref[0:1, lo:hi], res_ref[1:2, lo:hi], lo, hi
        )
        rows = cam_ref[:, lo:hi] * live[:, lo:hi]
        every = jnp.concatenate(
            [rows, first, second, cam_ids[:, lo:hi], jnp.zeros((3, hi - lo), F32)], 0
        )
        for at in range(lo, hi, 128):
            block = every[:, at - lo : at - lo + 128]
            if at < inner:
                i = at // 128
                in_ref[ROWS * i : ROWS * i + ROWS, :] = block[:ROWS]
            else:
                outer_ref[...] = block
                outer_chosen = ids_of(block)
                outer_chosen_ref[...] = outer_chosen
                outer_chosen_t_ref[...] = outer_chosen.T
                outer_sum_ref[...] = both_halves(start_terms(block, outer_chosen.T))


def ids_of(owned):
    return one_hot(owned[20:21].astype(jnp.int32), 128)


def spread_cams(owned, first, second):
    row = lax.broadcasted_iota(jnp.int32, owned.shape, 0)
    return owned * jnp.where(row < 9, first, jnp.where(row < 18, second, 0.0))


def halves(sums):
    return sums[0:9] + sums[9:18]


def start_terms(owned, chosen_t):
    row = lax.broadcasted_iota(jnp.int32, owned.shape, 0)
    squares = jnp.where(row < 18, owned * owned, 0.0)
    terms = jnp.concatenate([spread_cams(owned, owned[18:19], owned[19:20]), squares], 0)
    return collect(terms, chosen_t)


def both_halves(sums):
    sums = unstack(sums, 2)
    return jnp.concatenate([halves(sums[0:24]), halves(sums[24:48])], 0)


def inner_of(pay_ref):
    return pay_ref.shape[0] // ROWS * 128


def owned_of(pay_ref, lo, hi):
    rows = [pay_ref[ROWS * i : ROWS * i + ROWS, :] for i in range(lo // 128, hi // 128)]
    return jnp.concatenate([jnp.concatenate(rows, 1), jnp.zeros((24 - ROWS, hi - lo), F32)], 0)


def start_sum_kernel(pay_ref, outer_sum_ref, damp_ref, group_ref, chosen_ref, chosen_t_ref):
    sums = None
    for lo, hi in spans(inner_of(pay_ref)):
        owned = owned_of(pay_ref, lo, hi)
        chosen = ids_of(owned)
        chosen_ref[:, lo:hi] = chosen
        chosen_t = chosen.T
        chosen_t_ref[lo:hi, :] = chosen_t
        sums = added(sums, start_terms(owned, chosen_t))
    sums = both_halves(sums)
    block = jnp.concatenate([sums[0:9], sums[9:18] + damp_ref[...], outer_sum_ref[...]], 0)
    put_blocks(group_ref, block)


def twice(values):
    return pieces(jnp.concatenate([values, values, jnp.zeros((6, 128), F32)], 0), 2)


def apply_cams(owned, stacked, chosen):
    product = owned * fetch(stacked, chosen)
    row = lax.broadcasted_iota(jnp.int32, (8, owned.shape[1]), 0)
    middle = product[8:16]
    first = col_sum(product[0:8] + jnp.where(row == 0, middle, 0.0))
    second = col_sum(product[16:24] + jnp.where(row == 0, 0.0, middle))
    return first, second


def put_moved(in_ref, out_ref, pay_ref, chosen_ref, outer_ref, outer_chosen_ref, own, twin):
    stacked = twice(own)
    for lo, hi in spans(inner_of(pay_ref)):
        moved = apply_cams(owned_of(pay_ref, lo, hi), stacked, chosen_ref[:, lo:hi])
        in_ref[0:1, lo:hi], in_ref[1:2, lo:hi] = moved
    put_rows(out_ref, apply_cams(outer_ref[...], twice(twin), outer_chosen_ref[...]))


def put_blocks(group_ref, block):
    rows = block.shape[0]
    for at in range(0, group_ref.shape[0], rows):
        group_ref[at : at + rows, :] = block


def partner_block(partner_ref, group_ref, rows, count):
    partner = partner_ref[...]
    out = group_ref[0:count, :]
    for i in range(1, group_ref.shape[0] // rows):
        out = jnp.where(partner == i, group_ref[rows * i : rows * i + count, :], out)
    return out


def start_kernel(
    partner_ref, group_ref, sent_ref, outer_sum_ref, pay_ref, chosen_ref, outer_ref,
    outer_chosen_ref,
    in_ref, out_ref, rem_ref, pre_ref, dir_ref,
):
    theirs = partner_block(partner_ref, group_ref, 36, 36)
    sums = [sent_ref[0:18, :] + theirs[18:36], theirs[0:18] + outer_sum_ref[...]]
    for i in range(2):
        remainder = -sums[i][0:9]
        precond = 1.0 / sums[i][9:18]
        rem_ref[i] = remainder
        pre_ref[i] = precond
        dir_ref[i] = precond * remainder
    put_moved(
        in_ref, out_ref, pay_ref, chosen_ref, outer_ref, outer_chosen_ref, dir_ref[0], dir_ref[1]
    )


def point_side(
    in_ref, out_ref, placed_ref, chosen_ref, chosen_t_ref, inverse_ref, outer_ref,
    outer_chosen_t_ref, back_ref, outer_sum_ref, values,
):
    n = placed_ref.shape[1]
    inner = n - 128
    sums = None
    for lo, hi in spans(n):
        first, second = slots_of(in_ref, out_ref, 0, lo, hi), slots_of(in_ref, out_ref, 1, lo, hi)
        terms = spread_points(placed_ref, first, second, lo, hi)
        sums = added(sums, collect(terms, chosen_t_ref[lo:hi, :]))
    stacked = pieces(solve_points(inverse_ref[...], unstack(sums, 2)), 2)
    bend = None
    for lo, hi in spans(n):
        first, second = slots_of(in_ref, out_ref, 0, lo, hi), slots_of(in_ref, out_ref, 1, lo, hi)
        pulled = fetch(stacked, chosen_ref[:, lo:hi])
        kept = pull_points(placed_ref, pulled, first, second, lo, hi)
        bend = added(bend, lane_blocks(first * kept[0] + second * kept[1]))
        for at in range(lo, hi, 128):
            rows = [k[:, at - lo : at - lo + 128] for k in kept]
            if at < inner:
                i = 3 * (at // 128)
                back_ref[i : i + 1, :], back_ref[i + 1 : i + 2, :] = rows
            else:
                spread = spread_cams(outer_ref[...], *rows)
                outer = collect(spread, outer_chosen_t_ref[...])
                outer_sum_ref[...] = halves(unstack(outer, 2))
    values[1] = values[1] + total(bend)
    row = scalar_row(values)
    for i in range(inner // 128):
        back_ref[3 * i + 2 : 3 * i + 3, :] = row


def point_first_kernel(
    in_ref, out_ref, placed_ref, chosen_ref, chosen_t_ref, inverse_ref, outer_ref,
    outer_chosen_t_ref, damp_ref,
    rem_ref, dir_ref,
    back_ref, outer_sum_ref,
):
    direction = dir_ref[0]
    values = [total(rem_ref[0] * direction), total(damp_ref[...] * direction * direction)]
    point_side(
        in_ref, out_ref, placed_ref, chosen_ref, chosen_t_ref, inverse_ref, outer_ref,
        outer_chosen_t_ref, back_ref, outer_sum_ref, values,
    )


def point_next_kernel(
    in_ref, out_ref, placed_ref, chosen_ref, chosen_t_ref, inverse_ref, outer_ref,
    outer_chosen_t_ref, damp_ref,
    rem_ref, scaled_ref, image_ref,
    back_ref, outer_sum_ref,
):
    scaled = scaled_ref[0]
    values = [
        total(rem_ref[0] * scaled),
        total(damp_ref[...] * scaled * scaled),
        total(image_ref[...] * scaled),
    ]
    point_side(
        in_ref, out_ref, placed_ref, chosen_ref, chosen_t_ref, inverse_ref, outer_ref,
        outer_chosen_t_ref, back_ref, outer_sum_ref, values,
    )


def back_row(back_ref, r, lo, hi):
    rows = [back_ref[3 * i + r : 3 * i + r + 1, :] for i in range(lo // 128, hi // 128)]
    return jnp.concatenate(rows, 1)


def inner_image(back_ref, pay_ref, chosen_t_ref, damp_ref, field):
    sums = None
    row = None
    for lo, hi in spans(inner_of(pay_ref)):
        first, second = back_row(back_ref, 0, lo, hi), back_row(back_ref, 1, lo, hi)
        spread = spread_cams(owned_of(pay_ref, lo, hi), first, second)
        sums = added(sums, collect(spread, chosen_t_ref[lo:hi, :]))
        row = added(row, lane_blocks(back_row(back_ref, 2, lo, hi)))
    return damp_ref[...] * field + halves(unstack(sums, 2)), row


def image_kernel(back_ref, outer_sum_ref, pay_ref, chosen_t_ref, damp_ref, dir_ref, group_ref):
    image, partial = inner_image(back_ref, pay_ref, chosen_t_ref, damp_ref, dir_ref[0])
    put_blocks(group_ref, jnp.concatenate([image, outer_sum_ref[...], partial], 0))


def group_total(group_ref, r):
    row = group_ref[r : r + 1, :]
    for at in range(r + 1 + r, group_ref.shape[0], r + 1):
        row = row + group_ref[at : at + 1, :]
    return row


def camera_kernel(
    partner_ref, group_ref, sent_ref, outer_sum_ref, pay_ref, chosen_ref, outer_ref,
    outer_chosen_ref, rem_ref, pre_ref, dir_ref,
    in_ref, out_ref, next_rem_ref, scaled_ref, image_ref, sums_ref,
):
    sums = group_total(group_ref, 18)
    sums_ref[...] = sums
    norm, bend = scalars(sums, 2)
    step = norm / bend
    theirs = partner_block(partner_ref, group_ref, 19, 18)
    images = [sent_ref[0:9, :] + theirs[9:18], theirs[0:9] + outer_sum_ref[...]]
    image_ref[...] = images[0]
    for i in range(2):
        remainder = rem_ref[i] - step * images[i]
        next_rem_ref[i] = remainder
        scaled_ref[i] = pre_ref[i] * remainder
    put_moved(
        in_ref, out_ref, pay_ref, chosen_ref, outer_ref, outer_chosen_ref,
        scaled_ref[0], scaled_ref[1],
    )


def pair_kernel(
    back_ref, outer_sum_ref, pay_ref, chosen_t_ref, damp_ref, scaled_ref, group_ref, image_ref
):
    image, partial = inner_image(back_ref, pay_ref, chosen_t_ref, damp_ref, scaled_ref[0])
    image_ref[...] = image
    put_blocks(group_ref, jnp.concatenate([outer_sum_ref[...], partial], 0))


def last_kernel(
    partner_ref, group_ref, inner_ref, rem_ref, scaled_ref, dir_ref, image_ref, sums_ref,
    update_ref, next_rem_ref,
):
    norm, bend = scalars(sums_ref[...], 2)
    next_norm, next_bend, cross = scalars(group_total(group_ref, 9), 3)
    ratio = next_norm / norm
    next_bend = next_bend + ratio * (2.0 * cross + ratio * bend)
    step = next_norm / next_bend
    theirs = partner_block(partner_ref, group_ref, 10, 9)
    image = inner_ref[...] + theirs + ratio * image_ref[...]
    direction = dir_ref[0]
    update_ref[...] = norm / bend * direction + step * (scaled_ref[0] + ratio * direction)
    next_rem_ref[...] = rem_ref[0] - step * image


def call(kernel, name, shapes, *args):
    vmem = pl.BlockSpec(memory_space=pltpu.VMEM)
    return pl.pallas_call(
        kernel,
        name=name,
        out_shape=[jax.ShapeDtypeStruct(*shape) for shape in shapes],
        in_specs=[vmem] * len(args),
        out_specs=[vmem] * len(shapes),
        compiler_params=pltpu.CompilerParams(vmem_limit_bytes=32 * 1024 * 1024),
    )(*args)


def start(*args):
    n = args[0].shape[0]
    shapes = [
        ((ROWS * (n // 128 - 1), 128), F32),
        ((9, 128), F32),
        ((24, 128), F32),
        ((128, 128), BF16),
        ((128, 128), BF16),
        ((18, 128), F32),
        ((48, n), F32),
        ((48, 128), F32),
        ((128, n), BF16),
        ((n, 128), BF16),
        ((1, 128), jnp.int32),
    ]
    copies = [
        pltpu.SMEM(a.shape, a.dtype) if i == 1 else pltpu.VMEM(a.shape, a.dtype)
        for i, a in enumerate(args[:-1])
    ]
    args = [pltpu.with_memory_space_constraint(a, pltpu.HBM) for a in args[:-1]] + [args[-1]]
    return pl.pallas_call(
        setup_kernel,
        name="setup",
        out_shape=[jax.ShapeDtypeStruct(*shape) for shape in shapes],
        in_specs=[pl.BlockSpec(memory_space=pltpu.HBM)] * len(copies)
        + [pl.BlockSpec(memory_space=pltpu.SMEM)],
        out_specs=[pl.BlockSpec(memory_space=pltpu.VMEM)] * len(shapes),
        scratch_shapes=copies + [pltpu.SemaphoreType.DMA((len(copies),))],
        compiler_params=pltpu.CompilerParams(vmem_limit_bytes=32 * 1024 * 1024),
    )(*args)


def on_device(
    cam_jac, point_jac, residuals, obs_camera, obs_point, obs_count, cam_damp, pt_damp, partner_mask
):
    n = cam_jac.shape[1]
    inner = n - 128
    groups = lax.axis_size("group")

    def over_dev(values):
        return lax.all_to_all(values, "dev", split_axis=1, concat_axis=1, tiled=True)

    def rows_over_dev(values):
        blocks = values.reshape(inner // 128, -1, 1, 128)
        got = lax.all_to_all(blocks, "dev", split_axis=0, concat_axis=0, tiled=True)
        return got.reshape(values.shape)

    def over_group(values):
        blocks = values.reshape(groups, -1, 1, 128)
        got = lax.all_to_all(blocks, "group", split_axis=0, concat_axis=0, tiled=True)
        return got.reshape(values.shape)

    def sends(rows):
        return ((groups * rows, 128), F32)

    field, fields, line = ((9, 128), F32), ((2, 9, 128), F32), ((1, 128), F32)
    pair, back = [((2, inner), F32), ((2, 128), F32)], ((inner // 128 * 3, 128), F32)
    (
        pay, cam_damp, outer, outer_chosen, outer_chosen_t, outer_sum, placed, inverse,
        *ones, partner,
    ) = start(
        obs_point, obs_count, point_jac, residuals, pt_damp, cam_jac, obs_camera, cam_damp,
        partner_mask,
    )
    pay = rows_over_dev(pay)
    sums, chosen, chosen_t = call(
        start_sum_kernel, "start_sum", [sends(36), ((128, inner), BF16), ((inner, 128), BF16)],
        pay, outer_sum, cam_damp,
    )
    cameras = (pay, chosen, outer, outer_chosen)
    moved, outer_moved, remainder, precond, direction = call(
        start_kernel, "start", pair + [fields] * 3,
        partner, over_group(sums), sums, outer_sum, *cameras,
    )
    points = (placed, *ones, inverse, outer, outer_chosen_t, cam_damp)
    kept, outer_sum = call(
        point_first_kernel, "point_first", [back, field],
        over_dev(moved), outer_moved, *points, remainder, direction,
    )
    kept = rows_over_dev(kept)
    (images,) = call(
        image_kernel, "image", [sends(19)], kept, outer_sum, pay, chosen_t, cam_damp, direction
    )
    moved, outer_moved, remainder, scaled, image, totals = call(
        camera_kernel, "camera", pair + [fields] * 2 + [field, line],
        partner, over_group(images), images, outer_sum, *cameras, remainder, precond, direction,
    )
    kept, outer_sum = call(
        point_next_kernel, "point_next", [back, field],
        over_dev(moved), outer_moved, *points, remainder, scaled, image,
    )
    kept = rows_over_dev(kept)
    images, next_image = call(
        pair_kernel, "pair", [sends(10), field], kept, outer_sum, pay, chosen_t, cam_damp, scaled
    )
    update, remainder = call(
        last_kernel, "last", [field] * 2,
        partner, over_group(images), next_image, remainder, scaled, direction, image, totals,
    )
    return (update, remainder)


def solution(mesh):
    slots, rows = P(None, ("group", "dev")), P(("group", "dev"))
    return jax.shard_map(
        on_device,
        mesh=mesh,
        in_specs=(
            slots, slots, slots, rows, rows, P(("group", "dev"), None), slots, slots, P("dev"),
        ),
        out_specs=(slots, slots),
        check_vma=False,
    )
```
